32 devices in a mesh: seg: 8 (over y, x, core), band: 4 (over z).
Axes of the slice: x: 2, y: 2, z: 4, core: 2. Of those that a mesh axis runs over, the one named last changes fastest.
Arguments:
- jac_first: bfloat16 [8, 4, 4096, 384], P('seg', None, 'band'), may hold values from -0.09375 to 0.09375
- jac_second: bfloat16 [8, 4, 4096, 384], P('seg', None, 'band'), may hold values from -0.013671875 to 0.013671875
- residual: bfloat16 [8, 4, 4096], P('seg', None, 'band'), may hold values from -1.25 to 1.25
- damp_inner: float32 [8, 3, 384], P('seg'), may hold values from 0.01 to 0.05
- damp_sep: float32 [8, 384], P('seg'), may hold values from 0.01 to 0.05
Outputs:
- separators: float32 [8, 384], P('seg')
- interior: float32 [8, 3, 384], P('seg')
The draws below stay inside these ranges and needn't reach their ends.
All inputs are finite; a program needn't handle non-finite values.
Results may differ from the reference program's by a relative error of at most 0.0003.
Values may be sent and summed in bfloat16 or wider, within the bound.
A program may use at most 128 MiB of HBM per device.

```python
import math
import jax
import jax.numpy as jnp
from jax import lax

P_SIZE = 384
KB = 3
ROWS = 4096
LINKS = 4
SEGS = 8


def shard_levels(own_key, extent, shards, smallest, high):
    def one(dim, parts):
        steps = jax.random.uniform(jax.random.fold_in(jax.random.fold_in(own_key, 6), dim), (parts,), jnp.float32, smallest / len(shards), high / len(shards))
        return jnp.repeat(jnp.exp(steps), extent[dim] // parts).reshape((-1,) + (1,) * (len(extent) - dim - 1))

    factor_of = one(*shards[0])
    for cut in shards[1:]:
        factor_of = factor_of * one(*cut)
    return factor_of


def noise(stream_key, dims, scale, bound, shards=(), dtype=jnp.bfloat16):
    gain = shard_levels(stream_key, dims, shards, -0.22, 0.18) if shards else 1.0
    result = jax.random.normal(stream_key, dims, jnp.float32) * scale * gain
    return jnp.minimum(jnp.maximum(result, -bound), bound).astype(dtype)


def setup_inputs(seed: int = 0) -> dict:
    streams_of = jax.random.split(jax.random.key(seed), 6)
    jac_first = noise(streams_of[0], (SEGS, LINKS, ROWS, P_SIZE), ROWS ** -0.5, 0.09375, ((0, 8), (2, 4)))
    jac_second = noise(streams_of[1], (SEGS, LINKS, ROWS, P_SIZE), (0.15 / ROWS ** 0.5), 0.013671875, ((0, 8), (2, 4)))
    residual = noise(streams_of[2], (SEGS, LINKS, ROWS), 0.2, 1.25, ((0, 8), (2, 4)))
    damp_inner = jnp.clip(jnp.exp(math.log(0.05) - 1.609438 * jax.random.uniform(streams_of[3], (SEGS, KB, P_SIZE), jnp.float32) ** shard_levels(streams_of[3], (SEGS, KB, P_SIZE), ((0, 8),), -0.2, 0.2)), 0.01, 0.05)
    damp_sep = jnp.clip(jnp.exp(math.log(0.05) - 1.609438 * jax.random.uniform(streams_of[4], (SEGS, P_SIZE), jnp.float32) ** shard_levels(streams_of[4], (SEGS, P_SIZE), ((0, 8),), -0.2, 0.2)), 0.01, 0.05)
    return dict(jac_first=jac_first, jac_second=jac_second, residual=residual, damp_inner=damp_inner, damp_sep=damp_sep)


HIGH = lax.Precision.HIGHEST

def matmul_high(left, right):
    return jnp.matmul(left, right, precision=HIGH)

def lower_solve(chol, rhs):
    return jax.scipy.linalg.solve_triangular(chol, rhs, lower=True)

def upper_solve(chol, rhs):
    return jax.scipy.linalg.solve_triangular(chol, rhs, lower=True, trans=1)

def link_tiles(first, second, resid):
    first = first.astype(jnp.float32)
    second = second.astype(jnp.float32)
    resid = resid.astype(jnp.float32)
    paa = jnp.einsum('lri,lrj->lij', first, first, precision=HIGH)
    pab = jnp.einsum('lri,lrj->lij', first, second, precision=HIGH)
    pbb = jnp.einsum('lri,lrj->lij', second, second, precision=HIGH)
    grad_a = jnp.einsum('lri,lr->li', first, resid, precision=HIGH)
    grad_b = jnp.einsum('lri,lr->li', second, resid, precision=HIGH)
    size = paa.shape[-1]
    zero_tile = jnp.zeros((1, size, size), jnp.float32)
    zero_row = jnp.zeros((1, size), jnp.float32)
    diag = jnp.concatenate([paa, zero_tile]) + jnp.concatenate([zero_tile, pbb - pab - jnp.swapaxes(pab, 1, 2) + paa])
    off = pab - paa
    grad = jnp.concatenate([grad_a, zero_row]) + jnp.concatenate([zero_row, grad_b - grad_a])
    return (diag, off, grad)

def segment_complement(diag, off, grad, damp_inner, damp_sep):
    size = diag.shape[-1]
    inner = damp_inner.shape[0]
    chols, lows, zlist, wlist = ([], [], [], [])
    zero = jnp.zeros((size, size), jnp.float32)
    for k in range(inner):
        block = diag[k + 1] + jnp.diag(damp_inner[k])
        left = off[0].T if k == 0 else zero
        right = off[inner] if k == inner - 1 else zero
        couple = jnp.concatenate([left, right], axis=1)
        target = -grad[k + 1]
        if k > 0:
            block = block - matmul_high(lows[-1], lows[-1].T)
            couple = couple - matmul_high(lows[-1], zlist[-1])
            target = target - matmul_high(lows[-1], wlist[-1])
        chol = jnp.linalg.cholesky(block)
        zlist.append(lower_solve(chol, couple))
        wlist.append(lower_solve(chol, target))
        chols.append(chol)
        if k < inner - 1:
            lows.append(lower_solve(chol, off[k + 1]).T)
    top = jnp.concatenate([diag[0], zero], axis=1)
    bottom = jnp.concatenate([zero, diag[inner + 1] + jnp.diag(damp_sep)], axis=1)
    schur = jnp.concatenate([top, bottom], axis=0)
    reduced = jnp.concatenate([-grad[0], -grad[inner + 1]])
    for k in range(inner):
        schur = schur - matmul_high(zlist[k].T, zlist[k])
        reduced = reduced - matmul_high(zlist[k].T, wlist[k])
    comp = (schur[:size, :size], schur[:size, size:], schur[size:, size:], reduced[:size], reduced[size:])
    return (comp, (chols, lows, zlist, wlist))

def back_substitute(factors, left, right):
    chols, lows, zlist, wlist = factors
    inner = len(chols)
    ends = jnp.concatenate([left, right])
    values = [wlist[k] - matmul_high(zlist[k], ends) for k in range(inner)]
    steps = [None] * inner
    steps[inner - 1] = upper_solve(chols[inner - 1], values[inner - 1])
    for k in range(inner - 2, -1, -1):
        steps[k] = upper_solve(chols[k], values[k] - matmul_high(lows[k].T, steps[k + 1]))
    return jnp.stack(steps)

def merge(first_arc, second_arc):
    all_a, alr_a, arr_a, al_a, ar_a = first_arc
    bll, blr, brr, bl, br = second_arc
    size = all_a.shape[0]
    chol = jnp.linalg.cholesky(arr_a + bll)
    couple = jnp.concatenate([alr_a.T, blr], axis=1)
    weights = jax.scipy.linalg.cho_solve((chol, True), couple)
    shifted = jax.scipy.linalg.cho_solve((chol, True), ar_a + bl)
    new_ll = all_a - matmul_high(alr_a, weights[:, :size])
    new_lr = -matmul_high(alr_a, weights[:, size:])
    new_rr = brr - matmul_high(blr.T, weights[:, size:])
    new_l = al_a - matmul_high(alr_a, shifted)
    new_r = br - matmul_high(blr.T, shifted)
    return ((new_ll, new_lr, new_rr, new_l, new_r), (weights, shifted))

def closure(arc):
    all_a, alr_a, arr_a, al_a, ar_a = arc
    whole = all_a + alr_a + alr_a.T + arr_a
    chol = jnp.linalg.cholesky(whole)
    return jax.scipy.linalg.cho_solve((chol, True), al_a + ar_a)

def middle_step(saved, left, right):
    weights, shifted = saved
    size = left.shape[0]
    return shifted - matmul_high(weights[:, :size], left) - matmul_high(weights[:, size:], right)

def one_segment(items):
    first, second, resid, inner_damp, sep_damp = items
    diag, off, grad = link_tiles(first, second, resid)
    return segment_complement(diag, off, grad, inner_damp, sep_damp)

def reference(jac_first, jac_second, residual, damp_inner, damp_sep):
    comps, factors = lax.map(one_segment, (jac_first, jac_second, residual, damp_inner, damp_sep))
    count = jac_first.shape[0]
    levels = count.bit_length() - 1
    arcs = comps
    saved_all = []
    for level in range(levels):
        even = jax.tree.map(lambda item: item[0::2], arcs)
        odd = jax.tree.map(lambda item: item[1::2], arcs)
        arcs, saved = jax.vmap(merge)(even, odd)
        saved_all.append(saved)
    top = closure(jax.tree.map(lambda item: item[0], arcs))
    lefts = top[None]
    rights = top[None]
    for level in range(levels - 1, -1, -1):
        middles = jax.vmap(middle_step)(saved_all[level], lefts, rights)
        lefts = jnp.stack([lefts, middles], axis=1).reshape(-1, top.shape[0])
        rights = jnp.stack([middles, rights], axis=1).reshape(-1, top.shape[0])

    def solve_inner(items):
        factor, left, right = items
        return back_substitute(factor, left, right)
    interior = lax.map(solve_inner, (factors, lefts, rights))
    return (rights, interior)
```

```python
import functools

import jax
import jax.numpy as jnp
from jax import lax
from jax.experimental import pallas as pl
from jax.experimental.pallas import tpu as pltpu
from jax.sharding import PartitionSpec as P

HIGH = lax.Precision.HIGHEST
F32 = jnp.float32
BF16 = jnp.bfloat16
COARSE_STEPS = 8
FINE_STEPS = 64
FINE_ENOUGH = 1e-5
PAD = 8
VMEM_BYTES = 48 * 1024 * 1024


def mm(left, right):
    return jnp.dot(left, right, preferred_element_type=F32)


def mm_high(left, right):
    return jnp.dot(left, right, precision=HIGH, preferred_element_type=F32)


def mm_high_t(left, right):
    return lax.dot_general(
        left, right, (((1,), (1,)), ((), ())), precision=HIGH, preferred_element_type=F32
    )


def eye_mask(size):
    rows = lax.broadcasted_iota(jnp.int32, (size, size), 0)
    columns = lax.broadcasted_iota(jnp.int32, (size, size), 1)
    return rows == columns


def plus_diagonal(matrix, row):
    return matrix + jnp.where(eye_mask(matrix.shape[0]), row, 0.0)


def invert(mats, invs, resids):
    size = mats[0].shape[0]

    def start(m, x):
        scale = 1.0 / jnp.max(jnp.sum(jnp.abs(m[...]), axis=0, keepdims=True))
        x[...] = jnp.where(eye_mask(size), 2.0 * scale, 0.0) - (scale * scale) * m[...]

    def residual(m, x, r):
        r[...] = jnp.where(eye_mask(size), 1.0, 0.0) - mm_high(m[...], x[...])
        return jnp.sum(r[...] * r[...])

    def residuals():
        worst = None
        for m, x, r in zip(mats, invs, resids):
            one = residual(m, x, r)
            worst = one if worst is None else jnp.maximum(worst, one)
        return worst

    for m, x in zip(mats, invs):
        start(m, x)

    @pl.loop(0, COARSE_STEPS)
    def _(_):
        for m, x in zip(mats, invs):
            xb = x[...].astype(BF16)
            rb = jnp.where(eye_mask(size), 1.0, 0.0) - mm(m[...].astype(BF16), xb)
            x[...] += mm(xb, rb.astype(BF16))

    rho = residuals()
    good = rho < 0.25

    def keep():
        return rho

    def restart():
        for m, x in zip(mats, invs):
            start(m, x)
        return residuals()

    rho = lax.cond(good, keep, restart)

    def more(state):
        step, now = state
        return jnp.logical_and(step < FINE_STEPS, now > FINE_ENOUGH)

    def fine(state):
        step, _ = state
        for x, r in zip(invs, resids):
            x[...] += mm_high(x[...], r[...])
        return (step + 1, residuals())

    lax.while_loop(more, fine, (jnp.int32(0), rho))
    for x, r in zip(invs, resids):
        x[...] += mm_high(x[...], r[...])


def eliminate(inv, z, y, size):
    y[...] = mm_high(z[...], inv[...])
    ll = mm_high_t(y[:size, :], z[:size, :])
    lr = mm_high_t(y[:size, :], z[size : 2 * size, :])
    rr = mm_high_t(y[size : 2 * size, :], z[size : 2 * size, :])
    ends = mm_high_t(y[2 * size :, :], z[: 2 * size, :])
    return ll, lr, rr, ends[:1, :size], ends[:1, size:]


def put_couplings(z, from_left, from_right, target, size):
    z[:size, :] = from_left
    z[size : 2 * size, :] = from_right
    z[2 * size :, :] = jnp.zeros((PAD, size), F32)
    z[2 * size : 2 * size + 1, :] = target


def gram_kernel(first_ref, second_ref, resid_ref, out_ref, *, links, size):
    link = pl.program_id(0)
    first = first_ref[0]
    second = second_ref[0]
    both = jnp.concatenate([first, second], axis=1)
    at = first.T
    prod = mm(at, both)
    paa = prod[:, :size]
    pab = prod[:, size:]
    pbb = mm(second.T, second)
    grads = mm(resid_ref[0], both)[:1, :]
    grad_a = grads[:, :size]
    grad_b = grads[:, size:]
    tail = (2 * links + 1) * size

    @pl.when(link == 0)
    def _():
        out_ref[:size, :] = jnp.zeros((size, size), F32)
        out_ref[tail:, :] = jnp.zeros((PAD, size), F32)

    here = pl.multiple_of(link * size, size)
    out_ref[pl.ds(here, size), :] += paa
    out_ref[pl.ds(pl.multiple_of(here + size, size), size), :] = pbb - pab - pab.T + paa
    out_ref[pl.ds(pl.multiple_of(here + (links + 1) * size, size), size), :] = pab - paa
    rows = lax.broadcasted_iota(jnp.int32, (PAD, size), 0)
    out_ref[tail:, :] += jnp.where(rows == link, grad_a, 0.0) + jnp.where(
        rows == link + 1, grad_b - grad_a, 0.0
    )


def gram(first, second, resid):
    links, rows, size = first.shape
    height = (2 * links + 1) * size + PAD
    padded = jnp.broadcast_to(resid[:, None, :], (links, 16, rows))
    block = pl.BlockSpec((1, rows, size), lambda link: (link, 0, 0))
    return pl.pallas_call(
        functools.partial(gram_kernel, links=links, size=size),
        grid=(links,),
        in_specs=[block, block, pl.BlockSpec((1, 16, rows), lambda link: (link, 0, 0))],
        out_specs=pl.BlockSpec((height, size), lambda link: (0, 0)),
        out_shape=jax.ShapeDtypeStruct((height, size), F32),
        compiler_params=pltpu.CompilerParams(vmem_limit_bytes=VMEM_BYTES),
        name="gram",
    )(first, second, padded)


def segment_kernel(
    tiles_ref, inner_ref, sep_ref, arc_ref, y1_ref, y2_ref, y3_ref, m1, m3, x1, x3, r1, r3, z1, z3
):
    size = tiles_ref.shape[1]

    def tile(k):
        return tiles_ref[k * size : (k + 1) * size, :]

    def target(k):
        return -tiles_ref[9 * size + k : 9 * size + k + 1, :]

    m1[...] = plus_diagonal(tile(1), inner_ref[0:1, :])
    m3[...] = plus_diagonal(tile(3), inner_ref[2:3, :])
    put_couplings(z1, tile(5), tile(6).T, target(1), size)
    put_couplings(z3, tile(7), tile(8).T, target(3), size)
    invert([m1, m3], [x1, x3], [r1, r3])
    ll1, lr1, rr1, l1, e1 = eliminate(x1, z1, y1_ref, size)
    m1[...] = plus_diagonal(tile(2), inner_ref[1:2, :]) - rr1
    z1[:size, :] = -lr1
    arc_ref[:size, :] = tile(0) - ll1
    ll3, lr3, rr3, l3, e3 = eliminate(x3, z3, y3_ref, size)
    m1[...] -= ll3
    put_couplings(z1, z1[:size, :], -lr3.T, target(2) - e1 - l3, size)
    arc_ref[2 * size : 3 * size, :] = plus_diagonal(tile(4), sep_ref[0:1, :]) - rr3
    invert([m1], [x1], [r1])
    ll2, lr2, rr2, l2, e2 = eliminate(x1, z1, y2_ref, size)
    arc_ref[:size, :] -= ll2
    arc_ref[size : 2 * size, :] = -lr2
    arc_ref[2 * size : 3 * size, :] -= rr2
    arc_ref[3 * size :, :] = jnp.zeros((PAD, size), F32)
    arc_ref[3 * size : 3 * size + 1, :] = target(0) - l1 - l2
    arc_ref[3 * size + 1 : 3 * size + 2, :] = target(4) - e3 - e2


def segment(tiles, inner, sep):
    size = tiles.shape[1]
    square = pltpu.VMEM((size, size), F32)
    couplings = jax.ShapeDtypeStruct((2 * size + PAD, size), F32)
    tall = pltpu.VMEM((2 * size + PAD, size), F32)
    return pl.pallas_call(
        segment_kernel,
        out_shape=[jax.ShapeDtypeStruct((3 * size + PAD, size), F32)] + [couplings] * 3,
        scratch_shapes=[square] * 6 + [tall] * 2,
        compiler_params=pltpu.CompilerParams(vmem_limit_bytes=VMEM_BYTES),
        name="segment",
    )(tiles, inner, sep)


def merge_kernel(right_ref, mine_ref, other_ref, arc_ref, y_ref, m, x, r, z):
    size = mine_ref.shape[1]
    is_right = right_ref[0] == 1

    def first(low, high):
        return jnp.where(is_right, other_ref[low:high, :], mine_ref[low:high, :])

    def second(low, high):
        return jnp.where(is_right, mine_ref[low:high, :], other_ref[low:high, :])

    end = 3 * size
    m[...] = first(2 * size, end) + second(0, size)
    put_couplings(
        z,
        first(size, 2 * size),
        second(size, 2 * size).T,
        first(end + 1, end + 2) + second(end, end + 1),
        size,
    )
    invert([m], [x], [r])
    ll, lr, rr, left, right = eliminate(x, z, y_ref, size)
    arc_ref[:size, :] = first(0, size) - ll
    arc_ref[size : 2 * size, :] = -lr
    arc_ref[2 * size : end, :] = second(2 * size, end) - rr
    arc_ref[end:, :] = jnp.zeros((PAD, size), F32)
    arc_ref[end : end + 1, :] = first(end, end + 1) - left
    arc_ref[end + 1 : end + 2, :] = second(end + 1, end + 2) - right


def merge(is_right, mine, other):
    size = mine.shape[1]
    square = pltpu.VMEM((size, size), F32)
    vmem = pl.BlockSpec(memory_space=pltpu.VMEM)
    return pl.pallas_call(
        merge_kernel,
        in_specs=[pl.BlockSpec(memory_space=pltpu.SMEM), vmem, vmem],
        out_shape=[
            jax.ShapeDtypeStruct((3 * size + PAD, size), F32),
            jax.ShapeDtypeStruct((2 * size + PAD, size), F32),
        ],
        scratch_shapes=[square] * 3 + [pltpu.VMEM((2 * size + PAD, size), F32)],
        compiler_params=pltpu.CompilerParams(vmem_limit_bytes=VMEM_BYTES),
        name="merge",
    )(is_right, mine, other)


def finish_kernel(levels, bits_ref, arc_ref, *refs):
    merged = refs[:levels]
    y1_ref, y2_ref, y3_ref, sep_ref, inner_ref, m, x, r = refs[levels:]
    size = arc_ref.shape[1]
    end = 3 * size
    lr = arc_ref[size : 2 * size, :]
    m[...] = arc_ref[:size, :] + lr + lr.T + arc_ref[2 * size : end, :]
    invert([m], [x], [r])

    def middle(y_ref, left, right):
        return (
            y_ref[2 * size : 2 * size + PAD, :]
            - mm_high(left, y_ref[:size, :])
            - mm_high(right, y_ref[size : 2 * size, :])
        )

    total = arc_ref[end : end + 1, :] + arc_ref[end + 1 : end + 2, :]
    top = mm_high(jnp.broadcast_to(total, (PAD, size)), x[...])
    left, right = top, top
    for level in range(levels - 1, -1, -1):
        between = middle(merged[level], left, right)
        between = jnp.broadcast_to(between[:1, :], (PAD, size))
        in_right = bits_ref[level] == 1
        left, right = jnp.where(in_right, between, left), jnp.where(in_right, right, between)
    step2 = jnp.broadcast_to(middle(y2_ref, left, right)[:1, :], (PAD, size))
    step1 = middle(y1_ref, left, step2)
    step3 = middle(y3_ref, step2, right)
    sep_ref[...] = right[:1, :]
    inner_ref[0:1, :] = step1[:1, :]
    inner_ref[1:2, :] = step2[:1, :]
    inner_ref[2:3, :] = step3[:1, :]


def finish(bits, arc, merged, inner):
    size = arc.shape[1]
    square = pltpu.VMEM((size, size), F32)
    vmem = pl.BlockSpec(memory_space=pltpu.VMEM)
    return pl.pallas_call(
        functools.partial(finish_kernel, len(merged)),
        in_specs=[pl.BlockSpec(memory_space=pltpu.SMEM)] + [vmem] * (1 + len(merged) + len(inner)),
        out_shape=[
            jax.ShapeDtypeStruct((1, size), F32),
            jax.ShapeDtypeStruct((len(inner), size), F32),
        ],
        scratch_shapes=[square] * 3,
        compiler_params=pltpu.CompilerParams(vmem_limit_bytes=VMEM_BYTES),
        name="finish",
    )(bits, arc, *merged, *inner)


def shards(jac_first, jac_second, residual, damp_inner, damp_sep):
    tiles = lax.psum(gram(jac_first[0], jac_second[0], residual[0]), "band")
    arc, *inner = segment(tiles, damp_inner[0], damp_sep)
    count = lax.axis_size("seg")
    levels = count.bit_length() - 1
    here = lax.axis_index("seg")
    bits = jnp.stack([(here >> level) & 1 for level in range(levels)]).astype(jnp.int32)
    merged = []
    for level in range(levels):
        pairs = [(i, i ^ (1 << level)) for i in range(count)]
        other = lax.ppermute(arc, "seg", pairs)
        arc, saved = merge(bits[level : level + 1], arc, other)
        merged.append(saved)
    sep, steps = finish(bits, arc, merged, inner)
    return (sep, steps[None])


def solution(mesh):
    return jax.shard_map(
        shards,
        mesh=mesh,
        in_specs=(
            P("seg", None, "band", None),
            P("seg", None, "band", None),
            P("seg", None, "band"),
            P("seg", None, None),
            P("seg", None),
        ),
        out_specs=(P("seg", None), P("seg", None, None)),
        check_vma=False,
    )
```

```python
import functools

import jax
import jax.numpy as jnp
from jax import lax
from jax.experimental import pallas as pl
from jax.experimental.pallas import tpu as pltpu
from jax.sharding import PartitionSpec as P

HIGH = lax.Precision.HIGHEST
F32 = jnp.float32
BF16 = jnp.bfloat16
COARSE_STEPS = 5
FINE_STEPS = 64
FINE_ENOUGH = 1e-5
PAD = 8
TAIL = 16
CHUNK = 104
VMEM_BYTES = 48 * 1024 * 1024


def mm(left, right):
    return jnp.dot(left, right, preferred_element_type=F32)


def mm_high(left, right):
    return jnp.dot(left, right, precision=HIGH, preferred_element_type=F32)


def mm_high_t(left, right):
    return lax.dot_general(
        left, right, (((1,), (1,)), ((), ())), precision=HIGH, preferred_element_type=F32
    )


def eye_mask(size):
    rows = lax.broadcasted_iota(jnp.int32, (size, size), 0)
    columns = lax.broadcasted_iota(jnp.int32, (size, size), 1)
    return rows == columns


def plus_diagonal(matrix, row):
    return matrix + jnp.where(eye_mask(matrix.shape[0]), row, 0.0)


def diagonal_of(matrix):
    return jnp.sum(jnp.where(eye_mask(matrix.shape[0]), matrix, 0.0), axis=0, keepdims=True)


def lower_upper(low, up):
    size = low.shape[0]
    rows = lax.broadcasted_iota(jnp.int32, (size, size), 0)
    columns = lax.broadcasted_iota(jnp.int32, (size, size), 1)
    return jnp.where(rows > columns, low, jnp.where(rows < columns, up, 0.0))


def symmetric(half, diagonal):
    return plus_diagonal(half + half.T, diagonal)


def mm_three(left, right):
    lh, rh = left.astype(BF16), right.astype(BF16)
    ll, rl = (left - lh.astype(F32)).astype(BF16), (right - rh.astype(F32)).astype(BF16)
    return mm(lh, rh) + (mm(lh, rl) + mm(ll, rh))


def invert(mats, invs, resids):
    size = mats[0].shape[0]

    def start(m, x):
        scale = 1.0 / jnp.max(jnp.sum(jnp.abs(m[...]), axis=0, keepdims=True))
        x[...] = jnp.where(eye_mask(size), 2.0 * scale, 0.0) - (scale * scale) * m[...]

    def residuals(product):
        worst = None
        for m, x, r in zip(mats, invs, resids):
            r[...] = jnp.where(eye_mask(size), 1.0, 0.0) - product(m[...], x[...])
            one = jnp.sum(r[...] * r[...])
            worst = one if worst is None else jnp.maximum(worst, one)
        return worst

    for m, x in zip(mats, invs):
        start(m, x)

    @pl.loop(0, COARSE_STEPS)
    def _(_):
        for m, x in zip(mats, invs):
            xb = x[...].astype(BF16)
            rb = jnp.where(eye_mask(size), 1.0, 0.0) - mm(m[...].astype(BF16), xb)
            x[...] += mm(xb, rb.astype(BF16))

    good = residuals(mm_three) < 0.25

    @pl.when(good)
    def _():
        for x, r in zip(invs, resids):
            x[...] += mm(x[...].astype(BF16), r[...].astype(BF16))

    @pl.when(jnp.logical_not(good))
    def _():
        for m, x in zip(mats, invs):
            start(m, x)

    def more(state):
        step, now = state
        return jnp.logical_and(step < FINE_STEPS, now > FINE_ENOUGH)

    def fine(state):
        step, _ = state
        for x, r in zip(invs, resids):
            x[...] += mm_high(x[...], r[...])
        return (step + 1, residuals(mm_high))

    lax.while_loop(more, fine, (jnp.int32(0), residuals(mm_high)))
    for x, r in zip(invs, resids):
        x[...] += mm_three(x[...], r[...])


def eliminate(inv, z, y, size):
    y[...] = mm_high(z[...], inv[...])
    ll = mm_high_t(y[:size, :], z[:size, :])
    lr = mm_high_t(y[:size, :], z[size : 2 * size, :])
    rr = mm_high_t(y[size : 2 * size, :], z[size : 2 * size, :])
    ends = mm_high_t(y[2 * size :, :], z[: 2 * size, :])
    return ll, lr, rr, ends[:1, :size], ends[:1, size:]


def put_couplings(z, from_left, from_right, target, size):
    z[:size, :] = from_left
    z[size : 2 * size, :] = from_right
    z[2 * size :, :] = jnp.zeros((PAD, size), F32)
    z[2 * size : 2 * size + 1, :] = target


def gram_kernel(first_ref, second_ref, resid_ref, out_ref, *, links, size):
    link = pl.program_id(0)
    first = first_ref[0]
    second = second_ref[0]
    both = jnp.concatenate([first, second], axis=1)
    at = first.T
    prod = mm(at, both)
    paa = prod[:, :size]
    pab = prod[:, size:]
    pbb = mm(second.T, second)
    grads = mm(resid_ref[0], both)[:1, :]
    grad_a = grads[:, :size]
    grad_b = grads[:, size:]
    squares = links // 2 + 1
    tail = (squares + links) * size
    added = pbb - pab - pab.T + paa

    @pl.when(link == 0)
    def _():
        out_ref[: squares * size, :] = jnp.zeros((squares * size, size), F32)
        out_ref[tail:, :] = jnp.zeros((TAIL, size), F32)

    out_ref[pl.ds(pl.multiple_of((squares + link) * size, size), size), :] = pab - paa
    for k in range(links):

        @pl.when(link == k)
        def _(k=k):
            low, up = (paa, added) if k % 2 == 0 else (0.0 * paa, paa)
            at = k // 2 * size
            out_ref[at : at + size, :] += lower_upper(low, up)
            at += size
            if k == links - 1:
                out_ref[at : at + size, :] += added
            elif k % 2 == 1:
                out_ref[at : at + size, :] += lower_upper(added, 0.0 * paa)

    rows = lax.broadcasted_iota(jnp.int32, (TAIL, size), 0)
    out_ref[tail:, :] += (
        jnp.where(rows == link, diagonal_of(paa), 0.0)
        + jnp.where(rows == link + 1, diagonal_of(added), 0.0)
        + jnp.where(rows == link + PAD, grad_a, 0.0)
        + jnp.where(rows == link + PAD + 1, grad_b - grad_a, 0.0)
    )


def gram(first, second, resid):
    links, rows, size = first.shape
    height = (links // 2 + 1 + links) * size + TAIL
    padded = jnp.broadcast_to(resid[:, None, :], (links, 16, rows))
    block = pl.BlockSpec((1, rows, size), lambda link: (link, 0, 0))
    return pl.pallas_call(
        functools.partial(gram_kernel, links=links, size=size),
        grid=(links,),
        in_specs=[block, block, pl.BlockSpec((1, 16, rows), lambda link: (link, 0, 0))],
        out_specs=pl.BlockSpec((height, size), lambda link: (0, 0)),
        out_shape=jax.ShapeDtypeStruct((height, size), F32),
        compiler_params=pltpu.CompilerParams(vmem_limit_bytes=VMEM_BYTES),
        name="gram",
    )(first, second, padded)


def line_sum_kernel(axis, chunks, own, out, fl, fr, sr, sl, send_r, recv_r, send_l, recv_l):
    count = lax.axis_size(axis)
    me = lax.axis_index(axis)
    right, left = lax.rem(me + 1, count), lax.rem(me + count - 1, count)
    has_left, has_right = me > 0, me < count - 1
    barrier = pltpu.get_barrier_semaphore()

    @pl.when(has_left)
    def _():
        pl.semaphore_signal(
            barrier, inc=1, device_id={axis: left}, device_id_type=pl.DeviceIdType.MESH
        )

    @pl.when(has_right)
    def _():
        pl.semaphore_signal(
            barrier, inc=1, device_id={axis: right}, device_id_type=pl.DeviceIdType.MESH
        )

    @pl.when(jnp.logical_and(has_left, has_right))
    def _():
        pl.semaphore_wait(barrier, 2)

    @pl.when(jnp.logical_not(jnp.logical_and(has_left, has_right)))
    def _():
        pl.semaphore_wait(barrier, 1)

    def rows_of(chunk):
        return pl.ds(pl.multiple_of(chunk * CHUNK, 8), CHUNK)

    def copy(chunk, source, target, send, recv, device):
        rows = rows_of(chunk)
        return pltpu.make_async_remote_copy(
            src_ref=source.at[rows],
            dst_ref=target.at[rows],
            send_sem=send.at[chunk],
            recv_sem=recv.at[chunk],
            device_id={axis: device},
            device_id_type=pl.DeviceIdType.MESH,
        )

    def to_right(chunk):
        return copy(chunk, sr, fl, send_r, recv_r, right)

    def to_left(chunk):
        return copy(chunk, sl, fr, send_l, recv_l, left)

    def pass_on(chunk, there, source, came, has_in, has_out):
        rows = rows_of(chunk)

        @pl.when(has_in)
        def _():
            there(chunk).wait_recv()

        @pl.when(jnp.logical_and(has_in, has_out))
        def _():
            source[rows, :] = own[rows, :] + came[rows, :]
            there(chunk).start()

        @pl.when(jnp.logical_and(jnp.logical_not(has_in), has_out))
        def _():
            source[rows, :] = own[rows, :]
            there(chunk).start()

    def go_right(chunk):
        pass_on(chunk, to_right, sr, fl, has_left, has_right)

    def go_left(chunk):
        pass_on(chunk, to_left, sl, fr, has_right, has_left)

    near_left = 2 * me < count
    ahead = jnp.where(near_left, count - 1 - 2 * me, 2 * me + 1 - count)
    lag = 2 * ahead

    def step(i, carry):
        @pl.when(jnp.logical_and(i < chunks, near_left))
        def _():
            go_right(i)

        @pl.when(jnp.logical_and(i < chunks, jnp.logical_not(near_left)))
        def _():
            go_left(i)

        late = jnp.maximum(i - lag, 0)
        due = jnp.logical_and(i >= lag, i < chunks + lag)

        @pl.when(jnp.logical_and(due, near_left))
        def _():
            go_left(late)

        @pl.when(jnp.logical_and(due, jnp.logical_not(near_left)))
        def _():
            go_right(late)

        @pl.when(due)
        def _():
            rows = rows_of(late)

            @pl.when(jnp.logical_and(has_left, has_right))
            def _():
                out[rows, :] = fl[rows, :] + own[rows, :] + fr[rows, :]

            @pl.when(jnp.logical_not(has_left))
            def _():
                out[rows, :] = own[rows, :] + fr[rows, :]

            @pl.when(jnp.logical_not(has_right))
            def _():
                out[rows, :] = fl[rows, :] + own[rows, :]

        return carry

    lax.fori_loop(0, chunks + 2 * (count - 1), step, 0)

    def settle(chunk, carry):
        @pl.when(has_right)
        def _():
            to_right(chunk).wait_send()

        @pl.when(has_left)
        def _():
            to_left(chunk).wait_send()

        return carry

    lax.fori_loop(0, chunks, settle, 0)


def line_sum(own, axis):
    height, size = own.shape
    chunks = height // CHUNK
    assert height == chunks * CHUNK and lax.axis_size(axis) > 1
    return pl.pallas_call(
        functools.partial(line_sum_kernel, axis, chunks),
        in_specs=[pl.BlockSpec(memory_space=pltpu.VMEM)],
        out_specs=pl.BlockSpec(memory_space=pltpu.VMEM),
        out_shape=jax.ShapeDtypeStruct(own.shape, F32),
        scratch_shapes=[pltpu.VMEM(own.shape, F32)] * 4 + [pltpu.SemaphoreType.DMA((chunks,))] * 4,
        compiler_params=pltpu.CompilerParams(
            collective_id=0, has_side_effects=True, vmem_limit_bytes=VMEM_BYTES
        ),
        name="line_sum",
    )(own)


def put_arc(arc_ref, left, lr, right, left_diagonal, right_diagonal, l, r):
    size = lr.shape[0]
    end = 2 * size
    arc_ref[:size, :] = lower_upper(left, right)
    arc_ref[size:end, :] = lr
    arc_ref[end:, :] = jnp.zeros((PAD, size), F32)
    for k, row in enumerate((left_diagonal, right_diagonal, l, r)):
        arc_ref[end + k : end + k + 1, :] = row


def segment_kernel(
    tiles_ref, inner_ref, sep_ref, arc_ref, y1_ref, y2_ref, y3_ref, m1, m3, x1, x3, r1, r3, z1, z3
):
    size = tiles_ref.shape[1]

    tail = 7 * size

    def square(k):
        return tiles_ref[k * size : (k + 1) * size, :]

    def off(k):
        return square(3 + k)

    def diagonal(k):
        return tiles_ref[tail + k : tail + k + 1, :]

    def target(k):
        return -tiles_ref[tail + PAD + k : tail + PAD + k + 1, :]

    m1[...] = symmetric(lower_upper(jnp.zeros((size, size), F32), square(0)), diagonal(1) + inner_ref[0:1, :])
    m3[...] = symmetric(lower_upper(jnp.zeros((size, size), F32), square(1)), diagonal(3) + inner_ref[2:3, :])
    put_couplings(z1, off(0), off(1).T, target(1), size)
    put_couplings(z3, off(2), off(3).T, target(3), size)
    invert([m1, m3], [x1, x3], [r1, r3])
    ll1, lr1, rr1, l1, e1 = eliminate(x1, z1, y1_ref, size)
    m1[...] = symmetric(lower_upper(square(1), jnp.zeros((size, size), F32)), diagonal(2) + inner_ref[1:2, :]) - rr1
    z1[:size, :] = -lr1
    r1[...] = square(0) - ll1
    left_diagonal = diagonal(0) - diagonal_of(ll1)
    ll3, lr3, rr3, l3, e3 = eliminate(x3, z3, y3_ref, size)
    m1[...] -= ll3
    put_couplings(z1, z1[:size, :], -lr3.T, target(2) - e1 - l3, size)
    m3[...] = plus_diagonal(square(2), sep_ref[0:1, :]) - rr3
    x3[...] = r1[...]
    invert([m1], [x1], [r1])
    ll2, lr2, rr2, l2, e2 = eliminate(x1, z1, y2_ref, size)
    right = m3[...] - rr2
    put_arc(
        arc_ref,
        x3[...] - ll2,
        -lr2,
        right,
        left_diagonal - diagonal_of(ll2),
        diagonal_of(right),
        target(0) - l1 - l2,
        target(4) - e3 - e2,
    )


def segment(tiles, inner, sep):
    size = tiles.shape[1]
    square = pltpu.VMEM((size, size), F32)
    couplings = jax.ShapeDtypeStruct((2 * size + PAD, size), F32)
    tall = pltpu.VMEM((2 * size + PAD, size), F32)
    return pl.pallas_call(
        segment_kernel,
        out_shape=[jax.ShapeDtypeStruct((2 * size + PAD, size), F32)] + [couplings] * 3,
        scratch_shapes=[square] * 6 + [tall] * 2,
        compiler_params=pltpu.CompilerParams(vmem_limit_bytes=VMEM_BYTES),
        name="segment",
    )(tiles, inner, sep)


def merge_kernel(right_ref, mine_ref, other_ref, arc_ref, y_ref, m, x, r, z):
    size = mine_ref.shape[1]
    is_right = right_ref[0] == 1

    def first(low, high):
        return jnp.where(is_right, other_ref[low:high, :], mine_ref[low:high, :])

    def second(low, high):
        return jnp.where(is_right, mine_ref[low:high, :], other_ref[low:high, :])

    end = 2 * size

    def row(side, k):
        return side(end + k, end + k + 1)

    half = lower_upper(second(0, size), first(0, size))
    m[...] = symmetric(half, row(first, 1) + row(second, 0))
    put_couplings(
        z, first(size, end), second(size, end).T, row(first, 3) + row(second, 2), size
    )
    invert([m], [x], [r])
    ll, lr, rr, left, right = eliminate(x, z, y_ref, size)
    put_arc(
        arc_ref,
        first(0, size) - ll,
        -lr,
        second(0, size) - rr,
        row(first, 0) - diagonal_of(ll),
        row(second, 1) - diagonal_of(rr),
        row(first, 2) - left,
        row(second, 3) - right,
    )


def merge(is_right, mine, other):
    size = mine.shape[1]
    square = pltpu.VMEM((size, size), F32)
    vmem = pl.BlockSpec(memory_space=pltpu.VMEM)
    return pl.pallas_call(
        merge_kernel,
        in_specs=[pl.BlockSpec(memory_space=pltpu.SMEM), vmem, vmem],
        out_shape=[
            jax.ShapeDtypeStruct((2 * size + PAD, size), F32),
            jax.ShapeDtypeStruct((2 * size + PAD, size), F32),
        ],
        scratch_shapes=[square] * 3 + [pltpu.VMEM((2 * size + PAD, size), F32)],
        compiler_params=pltpu.CompilerParams(vmem_limit_bytes=VMEM_BYTES),
        name="merge",
    )(is_right, mine, other)


def finish_kernel(levels, bits_ref, arc_ref, *refs):
    merged = refs[:levels]
    y1_ref, y2_ref, y3_ref, sep_ref, inner_ref, m, x, r = refs[levels:]
    size = arc_ref.shape[1]
    end = 2 * size
    half = arc_ref[:size, :] + arc_ref[size:end, :]
    m[...] = symmetric(half, arc_ref[end : end + 1, :] + arc_ref[end + 1 : end + 2, :])
    invert([m], [x], [r])

    def middle(y_ref, left, right):
        return (
            y_ref[2 * size : 2 * size + PAD, :]
            - mm_high(left, y_ref[:size, :])
            - mm_high(right, y_ref[size : 2 * size, :])
        )

    total = arc_ref[end + 2 : end + 3, :] + arc_ref[end + 3 : end + 4, :]
    top = mm_high(jnp.broadcast_to(total, (PAD, size)), x[...])
    left, right = top, top
    for level in range(levels - 1, -1, -1):
        between = middle(merged[level], left, right)
        between = jnp.broadcast_to(between[:1, :], (PAD, size))
        in_right = bits_ref[level] == 1
        left, right = jnp.where(in_right, between, left), jnp.where(in_right, right, between)
    step2 = jnp.broadcast_to(middle(y2_ref, left, right)[:1, :], (PAD, size))
    step1 = middle(y1_ref, left, step2)
    step3 = middle(y3_ref, step2, right)
    sep_ref[...] = right[:1, :]
    inner_ref[0:1, :] = step1[:1, :]
    inner_ref[1:2, :] = step2[:1, :]
    inner_ref[2:3, :] = step3[:1, :]


def finish(bits, arc, merged, inner):
    size = arc.shape[1]
    square = pltpu.VMEM((size, size), F32)
    vmem = pl.BlockSpec(memory_space=pltpu.VMEM)
    return pl.pallas_call(
        functools.partial(finish_kernel, len(merged)),
        in_specs=[pl.BlockSpec(memory_space=pltpu.SMEM)] + [vmem] * (1 + len(merged) + len(inner)),
        out_shape=[
            jax.ShapeDtypeStruct((1, size), F32),
            jax.ShapeDtypeStruct((len(inner), size), F32),
        ],
        scratch_shapes=[square] * 3,
        compiler_params=pltpu.CompilerParams(vmem_limit_bytes=VMEM_BYTES),
        name="finish",
    )(bits, arc, *merged, *inner)


def shards(jac_first, jac_second, residual, damp_inner, damp_sep):
    tiles = line_sum(gram(jac_first[0], jac_second[0], residual[0]), "band")
    arc, *inner = segment(tiles, damp_inner[0], damp_sep)
    count = lax.axis_size("seg")
    levels = count.bit_length() - 1
    here = lax.axis_index("seg")
    bits = jnp.stack([(here >> level) & 1 for level in range(levels)]).astype(jnp.int32)
    merged = []
    for level in range(levels):
        pairs = [(i, i ^ (1 << level)) for i in range(count)]
        other = lax.ppermute(arc, "seg", pairs)
        arc, saved = merge(bits[level : level + 1], arc, other)
        merged.append(saved)
    sep, steps = finish(bits, arc, merged, inner)
    return (sep, steps[None])


def solution(mesh):
    return jax.shard_map(
        shards,
        mesh=mesh,
        in_specs=(
            P("seg", None, "band", None),
            P("seg", None, "band", None),
            P("seg", None, "band"),
            P("seg", None, None),
            P("seg", None),
        ),
        out_specs=(P("seg", None), P("seg", None, None)),
        check_vma=False,
    )
```

```python
import functools

import jax
import jax.numpy as jnp
from jax import lax
from jax.experimental import pallas as pl
from jax.experimental.pallas import tpu as pltpu
from jax.sharding import PartitionSpec as P

HIGH = lax.Precision.HIGHEST
F32 = jnp.float32
BF16 = jnp.bfloat16
COARSE_STEPS = 5
FINE_STEPS = 64
FINE_ENOUGH = 1e-5
PAD = 8
TAIL = 16
CHUNK = 56
ARC_PAD = 16
VMEM_BYTES = 48 * 1024 * 1024


def mm(left, right):
    return jnp.dot(left, right, preferred_element_type=F32)


def mm_high(left, right):
    return jnp.dot(left, right, precision=HIGH, preferred_element_type=F32)


def mm_high_t(left, right):
    return lax.dot_general(
        left, right, (((1,), (1,)), ((), ())), precision=HIGH, preferred_element_type=F32
    )


def eye_mask(size):
    rows = lax.broadcasted_iota(jnp.int32, (size, size), 0)
    columns = lax.broadcasted_iota(jnp.int32, (size, size), 1)
    return rows == columns


def plus_diagonal(matrix, row):
    return matrix + jnp.where(eye_mask(matrix.shape[0]), row, 0.0)


def diagonal_of(matrix):
    return jnp.sum(jnp.where(eye_mask(matrix.shape[0]), matrix, 0.0), axis=0, keepdims=True)


def lower_upper(low, up):
    size = low.shape[0]
    rows = lax.broadcasted_iota(jnp.int32, (size, size), 0)
    columns = lax.broadcasted_iota(jnp.int32, (size, size), 1)
    return jnp.where(rows > columns, low, jnp.where(rows < columns, up, 0.0))


def symmetric(half, diagonal):
    return plus_diagonal(half + half.T, diagonal)


def split(matrix):
    high = matrix.astype(BF16)
    return high, (matrix - high.astype(F32)).astype(BF16)


def mm_parts(left, right):
    return mm(left[0], right[0]) + (mm(left[0], right[1]) + mm(left[1], right[0]))


def mm_parts_t(left, right):
    def one(a, b):
        return lax.dot_general(a, b, (((1,), (1,)), ((), ())), preferred_element_type=F32)

    return one(left[0], right[0]) + (one(left[0], right[1]) + one(left[1], right[0]))


def mm_three(left, right):
    return mm_parts(split(left), split(right))


def invert(mats, invs, resids):
    size = mats[0].shape[0]

    def start(m, x):
        scale = 1.0 / jnp.max(jnp.sum(jnp.abs(m[...]), axis=0, keepdims=True))
        x[...] = jnp.where(eye_mask(size), 2.0 * scale, 0.0) - (scale * scale) * m[...]

    def residuals(product):
        worst = None
        for m, x, r in zip(mats, invs, resids):
            r[...] = jnp.where(eye_mask(size), 1.0, 0.0) - product(m[...], x[...])
            one = jnp.sum(r[...] * r[...])
            worst = one if worst is None else jnp.maximum(worst, one)
        return worst

    for m, x in zip(mats, invs):
        start(m, x)

    @pl.loop(0, COARSE_STEPS)
    def _(_):
        for m, x in zip(mats, invs):
            xb = x[...].astype(BF16)
            rb = jnp.where(eye_mask(size), 1.0, 0.0) - mm(m[...].astype(BF16), xb)
            x[...] += mm(xb, rb.astype(BF16))

    good = residuals(mm_three) < 0.25

    @pl.when(good)
    def _():
        for x, r in zip(invs, resids):
            x[...] += mm(x[...].astype(BF16), r[...].astype(BF16))

    @pl.when(jnp.logical_not(good))
    def _():
        for m, x in zip(mats, invs):
            start(m, x)

    def more(state):
        step, now = state
        return jnp.logical_and(step < FINE_STEPS, now > FINE_ENOUGH)

    def fine(state):
        step, _ = state
        for x, r in zip(invs, resids):
            x[...] += mm_high(x[...], r[...])
        return (step + 1, residuals(mm_high))

    lax.while_loop(more, fine, (jnp.int32(0), residuals(mm_high)))
    for x, r in zip(invs, resids):
        x[...] += mm_three(x[...], r[...])


def eliminate(inv, z, y, size):
    zs = split(z[...])
    y[...] = mm_parts(zs, split(inv[...]))
    ys = split(y[...])

    def rows(parts, low, high):
        return parts[0][low:high, :], parts[1][low:high, :]

    z_left, z_right = rows(zs, 0, size), rows(zs, size, 2 * size)
    y_left, y_right = rows(ys, 0, size), rows(ys, size, 2 * size)
    ll = mm_parts_t(y_left, z_left)
    lr = mm_parts_t(y_left, z_right)
    rr = mm_parts_t(y_right, z_right)
    solved = y[2 * size :, :]
    left = mm_high_t(solved, z[:size, :])
    right = mm_high_t(solved, z[size : 2 * size, :])
    return ll, lr, rr, left[:1, :], right[:1, :]


def put_couplings(z, from_left, from_right, target, size):
    z[:size, :] = from_left
    z[size : 2 * size, :] = from_right
    z[2 * size :, :] = jnp.zeros((PAD, size), F32)
    z[2 * size : 2 * size + 1, :] = target


def gram_kernel(first_ref, second_ref, resid_ref, out_ref, *, links, size):
    link = pl.program_id(0)
    first = first_ref[0]
    second = second_ref[0]
    both = jnp.concatenate([first, second], axis=1)
    at = first.T
    prod = mm(at, both)
    paa = prod[:, :size]
    pab = prod[:, size:]
    pbb = mm(second.T, second)
    grads = mm(resid_ref[0], both)[:1, :]
    grad_a = grads[:, :size]
    grad_b = grads[:, size:]
    third = size // 3
    strips = links // 2 * size
    offs = strips + 2 * third
    tail = offs + links * size
    added = pbb - pab - pab.T + paa

    @pl.when(link == 0)
    def _():
        out_ref[:offs, :] = jnp.zeros((offs, size), F32)
        out_ref[tail:, :] = jnp.zeros((TAIL, size), F32)

    out_ref[pl.ds(pl.multiple_of(offs + link * size, 8), size), :] = pab - paa
    for k in range(links):

        @pl.when(link == k)
        def _(k=k):
            low, up = (paa, added) if k % 2 == 0 else (0.0 * paa, paa)
            at = k // 2 * size
            out_ref[at : at + size, :] += lower_upper(low, up)
            at += size
            if k == links - 1:
                for strip, blocks in enumerate((((1, 0), (2, 0), (2, 1)), ((0, 0), (1, 1), (2, 2)))):
                    for place, (i, j) in enumerate(blocks):
                        out_ref[
                            at + strip * third : at + (strip + 1) * third,
                            place * third : (place + 1) * third,
                        ] = added[i * third : (i + 1) * third, j * third : (j + 1) * third]
            elif k % 2 == 1:
                out_ref[at : at + size, :] += lower_upper(added, 0.0 * paa)

    rows = lax.broadcasted_iota(jnp.int32, (TAIL, size), 0)
    out_ref[tail:, :] += (
        jnp.where(rows == link, diagonal_of(paa), 0.0)
        + jnp.where(rows == link + 1, diagonal_of(added), 0.0)
        + jnp.where(rows == link + PAD, grad_a, 0.0)
        + jnp.where(rows == link + PAD + 1, grad_b - grad_a, 0.0)
    )


def gram(first, second, resid):
    links, rows, size = first.shape
    height = (links // 2 + links) * size + 2 * (size // 3) + TAIL
    padded = jnp.broadcast_to(resid[:, None, :], (links, 16, rows))
    block = pl.BlockSpec((1, rows, size), lambda link: (link, 0, 0))
    return pl.pallas_call(
        functools.partial(gram_kernel, links=links, size=size),
        grid=(links,),
        in_specs=[block, block, pl.BlockSpec((1, 16, rows), lambda link: (link, 0, 0))],
        out_specs=pl.BlockSpec((height, size), lambda link: (0, 0)),
        out_shape=jax.ShapeDtypeStruct((height, size), F32),
        compiler_params=pltpu.CompilerParams(vmem_limit_bytes=VMEM_BYTES),
        name="gram",
    )(first, second, padded)


def line_sum_kernel(axis, chunks, own, out, fl, fr, sr, sl, send_r, recv_r, send_l, recv_l):
    count = lax.axis_size(axis)
    me = lax.axis_index(axis)
    right, left = lax.rem(me + 1, count), lax.rem(me + count - 1, count)
    has_left, has_right = me > 0, me < count - 1
    barrier = pltpu.get_barrier_semaphore()

    @pl.when(has_left)
    def _():
        pl.semaphore_signal(
            barrier, inc=1, device_id={axis: left}, device_id_type=pl.DeviceIdType.MESH
        )

    @pl.when(has_right)
    def _():
        pl.semaphore_signal(
            barrier, inc=1, device_id={axis: right}, device_id_type=pl.DeviceIdType.MESH
        )

    @pl.when(jnp.logical_and(has_left, has_right))
    def _():
        pl.semaphore_wait(barrier, 2)

    @pl.when(jnp.logical_not(jnp.logical_and(has_left, has_right)))
    def _():
        pl.semaphore_wait(barrier, 1)

    def rows_of(chunk):
        return pl.ds(pl.multiple_of(chunk * CHUNK, 8), CHUNK)

    def copy(chunk, source, target, send, recv, device):
        rows = rows_of(chunk)
        return pltpu.make_async_remote_copy(
            src_ref=source.at[rows],
            dst_ref=target.at[rows],
            send_sem=send.at[chunk],
            recv_sem=recv.at[chunk],
            device_id={axis: device},
            device_id_type=pl.DeviceIdType.MESH,
        )

    def to_right(chunk):
        return copy(chunk, sr, fl, send_r, recv_r, right)

    def to_left(chunk):
        return copy(chunk, sl, fr, send_l, recv_l, left)

    def pass_on(chunk, there, source, came, has_in, has_out):
        rows = rows_of(chunk)

        @pl.when(has_in)
        def _():
            there(chunk).wait_recv()

        @pl.when(jnp.logical_and(has_in, has_out))
        def _():
            source[rows, :] = own[rows, :] + came[rows, :]
            there(chunk).start()

        @pl.when(jnp.logical_and(jnp.logical_not(has_in), has_out))
        def _():
            source[rows, :] = own[rows, :]
            there(chunk).start()

    def go_right(chunk):
        pass_on(chunk, to_right, sr, fl, has_left, has_right)

    def go_left(chunk):
        pass_on(chunk, to_left, sl, fr, has_right, has_left)

    near_left = 2 * me < count
    ahead = jnp.where(near_left, count - 1 - 2 * me, 2 * me + 1 - count)
    lag = 2 * ahead

    def step(i, carry):
        @pl.when(jnp.logical_and(i < chunks, near_left))
        def _():
            go_right(i)

        @pl.when(jnp.logical_and(i < chunks, jnp.logical_not(near_left)))
        def _():
            go_left(i)

        late = jnp.maximum(i - lag, 0)
        due = jnp.logical_and(i >= lag, i < chunks + lag)

        @pl.when(jnp.logical_and(due, near_left))
        def _():
            go_left(late)

        @pl.when(jnp.logical_and(due, jnp.logical_not(near_left)))
        def _():
            go_right(late)

        @pl.when(due)
        def _():
            rows = rows_of(late)

            @pl.when(jnp.logical_and(has_left, has_right))
            def _():
                out[rows, :] = fl[rows, :] + own[rows, :] + fr[rows, :]

            @pl.when(jnp.logical_not(has_left))
            def _():
                out[rows, :] = own[rows, :] + fr[rows, :]

            @pl.when(jnp.logical_not(has_right))
            def _():
                out[rows, :] = fl[rows, :] + own[rows, :]

        return carry

    lax.fori_loop(0, chunks + 2 * (count - 1), step, 0)

    def settle(chunk, carry):
        @pl.when(has_right)
        def _():
            to_right(chunk).wait_send()

        @pl.when(has_left)
        def _():
            to_left(chunk).wait_send()

        return carry

    lax.fori_loop(0, chunks, settle, 0)


def line_sum(own, axis):
    height, size = own.shape
    chunks = height // CHUNK
    assert height == chunks * CHUNK and lax.axis_size(axis) > 1
    return pl.pallas_call(
        functools.partial(line_sum_kernel, axis, chunks),
        in_specs=[pl.BlockSpec(memory_space=pltpu.VMEM)],
        out_specs=pl.BlockSpec(memory_space=pltpu.VMEM),
        out_shape=jax.ShapeDtypeStruct(own.shape, F32),
        scratch_shapes=[pltpu.VMEM(own.shape, F32)] * 4 + [pltpu.SemaphoreType.DMA((chunks,))] * 4,
        compiler_params=pltpu.CompilerParams(
            collective_id=0, has_side_effects=True, vmem_limit_bytes=VMEM_BYTES
        ),
        name="line_sum",
    )(own)


def exchange_kernel(axis, bit, twin_axis, chunks, arc, out, land, send_a, recv_a, send_b, recv_b):
    me = lax.axis_index(axis)
    place = lax.axis_index(twin_axis)
    partner = me + bit - 2 * bit * ((me // bit) % 2)
    twin = place + 1 - 2 * (place % 2)
    base = (place % 2) * (chunks * CHUNK)
    barrier = pltpu.get_barrier_semaphore()
    for peer in ({axis: partner}, {twin_axis: twin}):
        pl.semaphore_signal(barrier, inc=1, device_id=peer, device_id_type=pl.DeviceIdType.MESH)
    pl.semaphore_wait(barrier, 2)

    def copy(chunk, source, send, recv, peer):
        rows = pl.ds(pl.multiple_of(base + chunk * CHUNK, 8), CHUNK)
        return pltpu.make_async_remote_copy(
            src_ref=source.at[rows],
            dst_ref=land.at[rows],
            send_sem=send.at[chunk],
            recv_sem=recv.at[chunk],
            device_id=peer,
            device_id_type=pl.DeviceIdType.MESH,
        )

    across = [copy(k, arc, send_a, recv_a, {axis: partner}) for k in range(chunks)]
    along = [copy(k, land, send_b, recv_b, {twin_axis: twin}) for k in range(chunks)]
    for one in across:
        one.start()
    for one, two in zip(across, along):
        one.wait_recv()
        two.start()
    for one, two in zip(across, along):
        two.wait_recv()
        one.wait_send()
        two.wait_send()
    out[...] = land[...]


def exchange(arc, axis, level, twin_axis):
    count, twins = lax.axis_size(axis), lax.axis_size(twin_axis)
    bit = 1 << level
    if level == 0 or twins % 2:
        return lax.ppermute(arc, axis, [(i, i ^ bit) for i in range(count)])
    chunks = arc.shape[0] // (2 * CHUNK)
    assert arc.shape[0] == 2 * chunks * CHUNK
    return pl.pallas_call(
        functools.partial(exchange_kernel, axis, bit, twin_axis, chunks),
        in_specs=[pl.BlockSpec(memory_space=pltpu.VMEM)],
        out_specs=pl.BlockSpec(memory_space=pltpu.VMEM),
        out_shape=jax.ShapeDtypeStruct(arc.shape, F32),
        scratch_shapes=[pltpu.VMEM(arc.shape, F32)] + [pltpu.SemaphoreType.DMA((chunks,))] * 4,
        compiler_params=pltpu.CompilerParams(
            collective_id=1 + level, has_side_effects=True, vmem_limit_bytes=VMEM_BYTES
        ),
        name=f"exchange_{level}",
    )(arc)


def put_arc(arc_ref, left, lr, right, left_diagonal, right_diagonal, l, r):
    size = lr.shape[0]
    end = 2 * size
    arc_ref[:size, :] = lower_upper(left, right)
    arc_ref[size:end, :] = lr
    arc_ref[end:, :] = jnp.zeros((ARC_PAD, size), F32)
    for k, row in enumerate((left_diagonal, right_diagonal, l, r)):
        arc_ref[end + k : end + k + 1, :] = row


def segment_kernel(
    tiles_ref, inner_ref, sep_ref, arc_ref, y1_ref, y2_ref, y3_ref, m1, m3, x1, x3, r1, r3, z1, z3
):
    size = tiles_ref.shape[1]

    third = size // 3
    offs = 2 * size + 2 * third
    tail = offs + 4 * size

    def square(k):
        return tiles_ref[k * size : (k + 1) * size, :]

    def off(k):
        return tiles_ref[offs + k * size : offs + (k + 1) * size, :]

    def strip(k, place):
        at = 2 * size + k * third
        return tiles_ref[at : at + third, place * third : (place + 1) * third]

    def put_last(ref):
        for place, (i, j) in enumerate(((1, 0), (2, 0), (2, 1))):
            block = strip(0, place)
            ref[i * third : (i + 1) * third, j * third : (j + 1) * third] = block
            ref[j * third : (j + 1) * third, i * third : (i + 1) * third] = block.T
            ref[place * third : (place + 1) * third, place * third : (place + 1) * third] = strip(
                1, place
            )

    def diagonal(k):
        return tiles_ref[tail + k : tail + k + 1, :]

    def target(k):
        return -tiles_ref[tail + PAD + k : tail + PAD + k + 1, :]

    m1[...] = symmetric(lower_upper(jnp.zeros((size, size), F32), square(0)), diagonal(1) + inner_ref[0:1, :])
    m3[...] = symmetric(lower_upper(jnp.zeros((size, size), F32), square(1)), diagonal(3) + inner_ref[2:3, :])
    put_couplings(z1, off(0), off(1).T, target(1), size)
    put_couplings(z3, off(2), off(3).T, target(3), size)
    invert([m1, m3], [x1, x3], [r1, r3])
    ll1, lr1, rr1, l1, e1 = eliminate(x1, z1, y1_ref, size)
    m1[...] = symmetric(lower_upper(square(1), jnp.zeros((size, size), F32)), diagonal(2) + inner_ref[1:2, :]) - rr1
    z1[:size, :] = -lr1
    r1[...] = square(0) - ll1
    left_diagonal = diagonal(0) - diagonal_of(ll1)
    ll3, lr3, rr3, l3, e3 = eliminate(x3, z3, y3_ref, size)
    m1[...] -= ll3
    put_couplings(z1, z1[:size, :], -lr3.T, target(2) - e1 - l3, size)
    put_last(m3)
    m3[...] = plus_diagonal(m3[...], sep_ref[0:1, :]) - rr3
    x3[...] = r1[...]
    invert([m1], [x1], [r1])
    ll2, lr2, rr2, l2, e2 = eliminate(x1, z1, y2_ref, size)
    right = m3[...] - rr2
    put_arc(
        arc_ref,
        x3[...] - ll2,
        -lr2,
        right,
        left_diagonal - diagonal_of(ll2),
        diagonal_of(right),
        target(0) - l1 - l2,
        target(4) - e3 - e2,
    )


def segment(tiles, inner, sep):
    size = tiles.shape[1]
    square = pltpu.VMEM((size, size), F32)
    couplings = jax.ShapeDtypeStruct((2 * size + PAD, size), F32)
    tall = pltpu.VMEM((2 * size + PAD, size), F32)
    return pl.pallas_call(
        segment_kernel,
        out_shape=[jax.ShapeDtypeStruct((2 * size + ARC_PAD, size), F32)] + [couplings] * 3,
        scratch_shapes=[square] * 6 + [tall] * 2,
        compiler_params=pltpu.CompilerParams(vmem_limit_bytes=VMEM_BYTES),
        name="segment",
    )(tiles, inner, sep)


def merge_kernel(right_ref, mine_ref, other_ref, arc_ref, y_ref, m, x, r, z):
    size = mine_ref.shape[1]
    is_right = right_ref[0] == 1

    def first(low, high):
        return jnp.where(is_right, other_ref[low:high, :], mine_ref[low:high, :])

    def second(low, high):
        return jnp.where(is_right, mine_ref[low:high, :], other_ref[low:high, :])

    end = 2 * size

    def row(side, k):
        return side(end + k, end + k + 1)

    half = lower_upper(second(0, size), first(0, size))
    m[...] = symmetric(half, row(first, 1) + row(second, 0))
    put_couplings(
        z, first(size, end), second(size, end).T, row(first, 3) + row(second, 2), size
    )
    invert([m], [x], [r])
    ll, lr, rr, left, right = eliminate(x, z, y_ref, size)
    put_arc(
        arc_ref,
        first(0, size) - ll,
        -lr,
        second(0, size) - rr,
        row(first, 0) - diagonal_of(ll),
        row(second, 1) - diagonal_of(rr),
        row(first, 2) - left,
        row(second, 3) - right,
    )


def merge(is_right, mine, other):
    size = mine.shape[1]
    square = pltpu.VMEM((size, size), F32)
    vmem = pl.BlockSpec(memory_space=pltpu.VMEM)
    return pl.pallas_call(
        merge_kernel,
        in_specs=[pl.BlockSpec(memory_space=pltpu.SMEM), vmem, vmem],
        out_shape=[
            jax.ShapeDtypeStruct((2 * size + ARC_PAD, size), F32),
            jax.ShapeDtypeStruct((2 * size + PAD, size), F32),
        ],
        scratch_shapes=[square] * 3 + [pltpu.VMEM((2 * size + PAD, size), F32)],
        compiler_params=pltpu.CompilerParams(vmem_limit_bytes=VMEM_BYTES),
        name="merge",
    )(is_right, mine, other)


def finish_kernel(levels, bits_ref, arc_ref, *refs):
    merged = refs[:levels]
    y1_ref, y2_ref, y3_ref, sep_ref, inner_ref, m, x, r = refs[levels:]
    size = arc_ref.shape[1]
    end = 2 * size
    half = arc_ref[:size, :] + arc_ref[size:end, :]
    m[...] = symmetric(half, arc_ref[end : end + 1, :] + arc_ref[end + 1 : end + 2, :])
    invert([m], [x], [r])

    def middle(y_ref, left, right):
        return (
            y_ref[2 * size : 2 * size + PAD, :]
            - mm_three(left, y_ref[:size, :])
            - mm_three(right, y_ref[size : 2 * size, :])
        )

    total = arc_ref[end + 2 : end + 3, :] + arc_ref[end + 3 : end + 4, :]
    top = mm_high(jnp.broadcast_to(total, (PAD, size)), x[...])
    left, right = top, top
    for level in range(levels - 1, -1, -1):
        between = middle(merged[level], left, right)
        between = jnp.broadcast_to(between[:1, :], (PAD, size))
        in_right = bits_ref[level] == 1
        left, right = jnp.where(in_right, between, left), jnp.where(in_right, right, between)
    step2 = jnp.broadcast_to(middle(y2_ref, left, right)[:1, :], (PAD, size))
    step1 = middle(y1_ref, left, step2)
    step3 = middle(y3_ref, step2, right)
    sep_ref[...] = right[:1, :]
    inner_ref[0:1, :] = step1[:1, :]
    inner_ref[1:2, :] = step2[:1, :]
    inner_ref[2:3, :] = step3[:1, :]


def finish(bits, arc, merged, inner):
    size = arc.shape[1]
    square = pltpu.VMEM((size, size), F32)
    vmem = pl.BlockSpec(memory_space=pltpu.VMEM)
    return pl.pallas_call(
        functools.partial(finish_kernel, len(merged)),
        in_specs=[pl.BlockSpec(memory_space=pltpu.SMEM)] + [vmem] * (1 + len(merged) + len(inner)),
        out_shape=[
            jax.ShapeDtypeStruct((1, size), F32),
            jax.ShapeDtypeStruct((len(inner), size), F32),
        ],
        scratch_shapes=[square] * 3,
        compiler_params=pltpu.CompilerParams(vmem_limit_bytes=VMEM_BYTES),
        name="finish",
    )(bits, arc, *merged, *inner)


def shards(jac_first, jac_second, residual, damp_inner, damp_sep):
    tiles = line_sum(gram(jac_first[0], jac_second[0], residual[0]), "band")
    arc, *inner = segment(tiles, damp_inner[0], damp_sep)
    count = lax.axis_size("seg")
    levels = count.bit_length() - 1
    here = lax.axis_index("seg")
    bits = jnp.stack([(here >> level) & 1 for level in range(levels)]).astype(jnp.int32)
    merged = []
    for level in range(levels):
        other = exchange(arc, "seg", level, "band")
        arc, saved = merge(bits[level : level + 1], arc, other)
        merged.append(saved)
    sep, steps = finish(bits, arc, merged, inner)
    return (sep, steps[None])


def solution(mesh):
    return jax.shard_map(
        shards,
        mesh=mesh,
        in_specs=(
            P("seg", None, "band", None),
            P("seg", None, "band", None),
            P("seg", None, "band"),
            P("seg", None, None),
            P("seg", None),
        ),
        out_specs=(P("seg", None), P("seg", None, None)),
        check_vma=False,
    )
```

```python
import functools

import jax
import jax.numpy as jnp
from jax import lax
from jax.experimental import pallas as pl
from jax.experimental.pallas import tpu as pltpu
from jax.sharding import PartitionSpec as P

HIGH = lax.Precision.HIGHEST
F32 = jnp.float32
BF16 = jnp.bfloat16
FINE_STEPS = 64
FINE_ENOUGH = 1e-6
PAD = 8
TAIL = 16
CHUNK = 56
ARC_PAD = 16
VMEM_BYTES = 48 * 1024 * 1024


def mm(left, right):
    return jnp.dot(left, right, preferred_element_type=F32)


def mm_high(left, right):
    return jnp.dot(left, right, precision=HIGH, preferred_element_type=F32)


def mm_high_t(left, right):
    return lax.dot_general(
        left, right, (((1,), (1,)), ((), ())), precision=HIGH, preferred_element_type=F32
    )


def eye_mask(size):
    rows = lax.broadcasted_iota(jnp.int32, (size, size), 0)
    columns = lax.broadcasted_iota(jnp.int32, (size, size), 1)
    return rows == columns


def plus_diagonal(matrix, row):
    return matrix + jnp.where(eye_mask(matrix.shape[0]), row, 0.0)


def diagonal_of(matrix):
    return jnp.sum(jnp.where(eye_mask(matrix.shape[0]), matrix, 0.0), axis=0, keepdims=True)


def lower_upper(low, up):
    size = low.shape[0]
    rows = lax.broadcasted_iota(jnp.int32, (size, size), 0)
    columns = lax.broadcasted_iota(jnp.int32, (size, size), 1)
    return jnp.where(rows > columns, low, jnp.where(rows < columns, up, 0.0))


def symmetric(half, diagonal):
    return plus_diagonal(half + half.T, diagonal)


def split(matrix):
    high = matrix.astype(BF16)
    return high, (matrix - high.astype(F32)).astype(BF16)


def mm_parts(left, right):
    return mm(
        jnp.concatenate([left[0], left[0], left[1]], axis=1),
        jnp.concatenate([right[0], right[1], right[0]], axis=0),
    )


def mm_parts_t(left, right):
    return lax.dot_general(
        jnp.concatenate([left[0], left[0], left[1]], axis=1),
        jnp.concatenate([right[0], right[1], right[0]], axis=1),
        (((1,), (1,)), ((), ())),
        preferred_element_type=F32,
    )


def mm_three(left, right):
    return mm_parts(split(left), split(right))


def invert(mats, invs, resids, coarse_steps):
    size = mats[0].shape[0]

    def start(m, x):
        scale = 1.0 / jnp.max(jnp.sum(jnp.abs(m[...]), axis=0, keepdims=True))
        x[...] = jnp.where(eye_mask(size), 2.0 * scale, 0.0) - (scale * scale) * m[...]

    def residuals(product):
        worst = None
        for m, x, r in zip(mats, invs, resids):
            r[...] = jnp.where(eye_mask(size), 1.0, 0.0) - product(m[...], x[...])
            one = jnp.sum(r[...] * r[...])
            worst = one if worst is None else jnp.maximum(worst, one)
        return worst

    for m, x in zip(mats, invs):
        start(m, x)

    @pl.loop(0, coarse_steps)
    def _(_):
        for m, x in zip(mats, invs):
            xb = x[...].astype(BF16)
            rb = jnp.where(eye_mask(size), 1.0, 0.0) - mm(m[...].astype(BF16), xb)
            x[...] += mm(xb, rb.astype(BF16))

    good = residuals(mm_three) < 0.25

    @pl.when(good)
    def _():
        for x, r in zip(invs, resids):
            x[...] += mm(x[...].astype(BF16), r[...].astype(BF16))

    @pl.when(jnp.logical_not(good))
    def _():
        for m, x in zip(mats, invs):
            start(m, x)

    def more(state):
        step, now = state
        return jnp.logical_and(step < FINE_STEPS, now > FINE_ENOUGH)

    def fine(state):
        step, _ = state
        for x, r in zip(invs, resids):
            x[...] += mm_high(x[...], r[...])
        return (step + 1, residuals(mm_high))

    lax.while_loop(more, fine, (jnp.int32(0), residuals(mm_high)))
    for x, r in zip(invs, resids):
        x[...] += mm(x[...].astype(BF16), r[...].astype(BF16))


def eliminate(inv, z, y, size):
    zs = split(z[...])
    y[...] = mm_parts(zs, split(inv[...]))
    ys = split(y[...])

    def rows(parts, low, high):
        return parts[0][low:high, :], parts[1][low:high, :]

    z_both, z_right = rows(zs, 0, 2 * size), rows(zs, size, 2 * size)
    y_left, y_right = rows(ys, 0, size), rows(ys, size, 2 * size)
    top = mm_parts_t(y_left, z_both)
    ll, lr = top[:, :size], top[:, size:]
    rr = mm_parts_t(y_right, z_right)
    solved = y[2 * size :, :]
    left = mm_high_t(solved, z[:size, :])
    right = mm_high_t(solved, z[size : 2 * size, :])
    return ll, lr, rr, left[:1, :], right[:1, :]


def put_couplings(z, from_left, from_right, target, size):
    z[:size, :] = from_left
    z[size : 2 * size, :] = from_right
    z[2 * size :, :] = jnp.zeros((PAD, size), F32)
    z[2 * size : 2 * size + 1, :] = target


def gram_kernel(first_ref, second_ref, resid_ref, out_ref, *, links, size):
    link = pl.program_id(0)
    first = first_ref[0]
    second = second_ref[0]
    both = jnp.concatenate([first, second], axis=1)
    at = first.T
    prod = mm(at, both)
    paa = prod[:, :size]
    pab = prod[:, size:]
    pbb = mm(second.T, second)
    grads = mm(resid_ref[...], both)
    which = lax.broadcasted_iota(jnp.int32, grads.shape, 0)
    grads = jnp.sum(jnp.where(which == link, grads, 0.0), axis=0, keepdims=True)
    grad_a = grads[:, :size]
    grad_b = grads[:, size:]
    third = size // 3
    strips = links // 2 * size
    offs = strips + 2 * third
    tail = offs + links * size
    added = pbb - pab - pab.T + paa

    @pl.when(link == 0)
    def _():
        out_ref[:offs, :] = jnp.zeros((offs, size), F32)
        out_ref[tail:, :] = jnp.zeros((TAIL, size), F32)

    out_ref[pl.ds(pl.multiple_of(offs + link * size, 8), size), :] = pab - paa
    for k in range(links):

        @pl.when(link == k)
        def _(k=k):
            low, up = (paa, added) if k % 2 == 0 else (0.0 * paa, paa)
            at = k // 2 * size
            out_ref[at : at + size, :] += lower_upper(low, up)
            at += size
            if k == links - 1:
                for strip, blocks in enumerate((((1, 0), (2, 0), (2, 1)), ((0, 0), (1, 1), (2, 2)))):
                    for place, (i, j) in enumerate(blocks):
                        out_ref[
                            at + strip * third : at + (strip + 1) * third,
                            place * third : (place + 1) * third,
                        ] = added[i * third : (i + 1) * third, j * third : (j + 1) * third]
            elif k % 2 == 1:
                out_ref[at : at + size, :] += lower_upper(added, 0.0 * paa)

    rows = lax.broadcasted_iota(jnp.int32, (TAIL, size), 0)
    out_ref[tail:, :] += (
        jnp.where(rows == link, diagonal_of(paa), 0.0)
        + jnp.where(rows == link + 1, diagonal_of(added), 0.0)
        + jnp.where(rows == link + PAD, grad_a, 0.0)
        + jnp.where(rows == link + PAD + 1, grad_b - grad_a, 0.0)
    )


def gram(first, second, resid):
    links, rows, size = first.shape
    height = (links // 2 + links) * size + 2 * (size // 3) + TAIL
    block = pl.BlockSpec((1, rows, size), lambda link: (link, 0, 0))
    return pl.pallas_call(
        functools.partial(gram_kernel, links=links, size=size),
        grid=(links,),
        in_specs=[block, block, pl.BlockSpec((links, rows), lambda link: (0, 0))],
        out_specs=pl.BlockSpec((height, size), lambda link: (0, 0)),
        out_shape=jax.ShapeDtypeStruct((height, size), F32),
        compiler_params=pltpu.CompilerParams(vmem_limit_bytes=VMEM_BYTES),
        name="gram",
    )(first, second, resid)


def line_sum_kernel(axis, chunks, own, out, fl, fr, sr, sl, send_r, recv_r, send_l, recv_l):
    count = lax.axis_size(axis)
    me = lax.axis_index(axis)
    right, left = lax.rem(me + 1, count), lax.rem(me + count - 1, count)
    has_left, has_right = me > 0, me < count - 1
    barrier = pltpu.get_barrier_semaphore()

    @pl.when(has_left)
    def _():
        pl.semaphore_signal(
            barrier, inc=1, device_id={axis: left}, device_id_type=pl.DeviceIdType.MESH
        )

    @pl.when(has_right)
    def _():
        pl.semaphore_signal(
            barrier, inc=1, device_id={axis: right}, device_id_type=pl.DeviceIdType.MESH
        )

    @pl.when(jnp.logical_and(has_left, has_right))
    def _():
        pl.semaphore_wait(barrier, 2)

    @pl.when(jnp.logical_not(jnp.logical_and(has_left, has_right)))
    def _():
        pl.semaphore_wait(barrier, 1)

    def rows_of(chunk):
        return pl.ds(pl.multiple_of(chunk * CHUNK, 8), CHUNK)

    def copy(chunk, source, target, send, recv, device):
        rows = rows_of(chunk)
        return pltpu.make_async_remote_copy(
            src_ref=source.at[rows],
            dst_ref=target.at[rows],
            send_sem=send.at[chunk],
            recv_sem=recv.at[chunk],
            device_id={axis: device},
            device_id_type=pl.DeviceIdType.MESH,
        )

    def to_right(chunk):
        return copy(chunk, sr, fl, send_r, recv_r, right)

    def to_left(chunk):
        return copy(chunk, sl, fr, send_l, recv_l, left)

    def pass_on(chunk, there, source, came, has_in, has_out):
        rows = rows_of(chunk)

        @pl.when(has_in)
        def _():
            there(chunk).wait_recv()

        @pl.when(jnp.logical_and(has_in, has_out))
        def _():
            source[rows, :] = own[rows, :] + came[rows, :]
            there(chunk).start()

        @pl.when(jnp.logical_and(jnp.logical_not(has_in), has_out))
        def _():
            source[rows, :] = own[rows, :]
            there(chunk).start()

    def go_right(chunk):
        pass_on(chunk, to_right, sr, fl, has_left, has_right)

    def go_left(chunk):
        pass_on(chunk, to_left, sl, fr, has_right, has_left)

    near_left = 2 * me < count
    ahead = jnp.where(near_left, count - 1 - 2 * me, 2 * me + 1 - count)
    lag = 2 * ahead

    def step(i, carry):
        @pl.when(jnp.logical_and(i < chunks, near_left))
        def _():
            go_right(i)

        @pl.when(jnp.logical_and(i < chunks, jnp.logical_not(near_left)))
        def _():
            go_left(i)

        late = jnp.maximum(i - lag, 0)
        due = jnp.logical_and(i >= lag, i < chunks + lag)

        @pl.when(jnp.logical_and(due, near_left))
        def _():
            go_left(late)

        @pl.when(jnp.logical_and(due, jnp.logical_not(near_left)))
        def _():
            go_right(late)

        @pl.when(due)
        def _():
            rows = rows_of(late)

            @pl.when(jnp.logical_and(has_left, has_right))
            def _():
                out[rows, :] = fl[rows, :] + own[rows, :] + fr[rows, :]

            @pl.when(jnp.logical_not(has_left))
            def _():
                out[rows, :] = own[rows, :] + fr[rows, :]

            @pl.when(jnp.logical_not(has_right))
            def _():
                out[rows, :] = fl[rows, :] + own[rows, :]

        return carry

    lax.fori_loop(0, chunks + 2 * (count - 1), step, 0)

    def settle(chunk, carry):
        @pl.when(has_right)
        def _():
            to_right(chunk).wait_send()

        @pl.when(has_left)
        def _():
            to_left(chunk).wait_send()

        return carry

    lax.fori_loop(0, chunks, settle, 0)


def line_sum(own, axis):
    height, size = own.shape
    chunks = height // CHUNK
    assert height == chunks * CHUNK and lax.axis_size(axis) > 1
    return pl.pallas_call(
        functools.partial(line_sum_kernel, axis, chunks),
        in_specs=[pl.BlockSpec(memory_space=pltpu.VMEM)],
        out_specs=pl.BlockSpec(memory_space=pltpu.VMEM),
        out_shape=jax.ShapeDtypeStruct(own.shape, F32),
        scratch_shapes=[pltpu.VMEM(own.shape, F32)] * 4 + [pltpu.SemaphoreType.DMA((chunks,))] * 4,
        compiler_params=pltpu.CompilerParams(
            collective_id=0, has_side_effects=True, vmem_limit_bytes=VMEM_BYTES
        ),
        name="line_sum",
    )(own)


def exchange_kernel(axis, bit, twin_axis, chunks, arc, out, land, send_a, recv_a, send_b, recv_b):
    me = lax.axis_index(axis)
    place = lax.axis_index(twin_axis)
    partner = me + bit - 2 * bit * ((me // bit) % 2)
    twin = place + 1 - 2 * (place % 2)
    base = (place % 2) * (chunks * CHUNK)
    barrier = pltpu.get_barrier_semaphore()
    for peer in ({axis: partner}, {twin_axis: twin}):
        pl.semaphore_signal(barrier, inc=1, device_id=peer, device_id_type=pl.DeviceIdType.MESH)
    pl.semaphore_wait(barrier, 2)

    def copy(chunk, source, send, recv, peer):
        rows = pl.ds(pl.multiple_of(base + chunk * CHUNK, 8), CHUNK)
        return pltpu.make_async_remote_copy(
            src_ref=source.at[rows],
            dst_ref=land.at[rows],
            send_sem=send.at[chunk],
            recv_sem=recv.at[chunk],
            device_id=peer,
            device_id_type=pl.DeviceIdType.MESH,
        )

    across = [copy(k, arc, send_a, recv_a, {axis: partner}) for k in range(chunks)]
    along = [copy(k, land, send_b, recv_b, {twin_axis: twin}) for k in range(chunks)]
    for one in across:
        one.start()
    for one, two in zip(across, along):
        one.wait_recv()
        two.start()
    for one, two in zip(across, along):
        two.wait_recv()
        one.wait_send()
        two.wait_send()
    out[...] = land[...]


def exchange(arc, axis, level, twin_axis):
    count, twins = lax.axis_size(axis), lax.axis_size(twin_axis)
    bit = 1 << level
    if level == 0 or twins % 2:
        return lax.ppermute(arc, axis, [(i, i ^ bit) for i in range(count)])
    chunks = arc.shape[0] // (2 * CHUNK)
    assert arc.shape[0] == 2 * chunks * CHUNK
    return pl.pallas_call(
        functools.partial(exchange_kernel, axis, bit, twin_axis, chunks),
        in_specs=[pl.BlockSpec(memory_space=pltpu.VMEM)],
        out_specs=pl.BlockSpec(memory_space=pltpu.VMEM),
        out_shape=jax.ShapeDtypeStruct(arc.shape, F32),
        scratch_shapes=[pltpu.VMEM(arc.shape, F32)] + [pltpu.SemaphoreType.DMA((chunks,))] * 4,
        compiler_params=pltpu.CompilerParams(
            collective_id=1 + level, has_side_effects=True, vmem_limit_bytes=VMEM_BYTES
        ),
        name=f"exchange_{level}",
    )(arc)


def put_arc(arc_ref, left, lr, right, left_diagonal, right_diagonal, l, r):
    size = lr.shape[0]
    end = 2 * size
    arc_ref[:size, :] = lower_upper(left, right)
    arc_ref[size:end, :] = lr
    arc_ref[end:, :] = jnp.zeros((ARC_PAD, size), F32)
    for k, row in enumerate((left_diagonal, right_diagonal, l, r)):
        arc_ref[end + k : end + k + 1, :] = row


def segment_kernel(
    tiles_ref, inner_ref, sep_ref, arc_ref, y1_ref, y2_ref, y3_ref, m1, m3, x1, x3, r1, r3, z1, z3
):
    size = tiles_ref.shape[1]

    third = size // 3
    offs = 2 * size + 2 * third
    tail = offs + 4 * size

    def square(k):
        return tiles_ref[k * size : (k + 1) * size, :]

    def off(k):
        return tiles_ref[offs + k * size : offs + (k + 1) * size, :]

    def strip(k, place):
        at = 2 * size + k * third
        return tiles_ref[at : at + third, place * third : (place + 1) * third]

    def put_last(ref):
        for place, (i, j) in enumerate(((1, 0), (2, 0), (2, 1))):
            block = strip(0, place)
            ref[i * third : (i + 1) * third, j * third : (j + 1) * third] = block
            ref[j * third : (j + 1) * third, i * third : (i + 1) * third] = block.T
            ref[place * third : (place + 1) * third, place * third : (place + 1) * third] = strip(
                1, place
            )

    def diagonal(k):
        return tiles_ref[tail + k : tail + k + 1, :]

    def target(k):
        return -tiles_ref[tail + PAD + k : tail + PAD + k + 1, :]

    m1[...] = symmetric(lower_upper(jnp.zeros((size, size), F32), square(0)), diagonal(1) + inner_ref[0:1, :])
    m3[...] = symmetric(lower_upper(jnp.zeros((size, size), F32), square(1)), diagonal(3) + inner_ref[2:3, :])
    put_couplings(z1, off(0), off(1).T, target(1), size)
    put_couplings(z3, off(2), off(3).T, target(3), size)
    invert([m1, m3], [x1, x3], [r1, r3], 4)
    ll1, lr1, rr1, l1, e1 = eliminate(x1, z1, y1_ref, size)
    m1[...] = symmetric(lower_upper(square(1), jnp.zeros((size, size), F32)), diagonal(2) + inner_ref[1:2, :]) - rr1
    z1[:size, :] = -lr1
    r1[...] = square(0) - ll1
    left_diagonal = diagonal(0) - diagonal_of(ll1)
    ll3, lr3, rr3, l3, e3 = eliminate(x3, z3, y3_ref, size)
    m1[...] -= ll3
    put_couplings(z1, z1[:size, :], -lr3.T, target(2) - e1 - l3, size)
    put_last(m3)
    m3[...] = plus_diagonal(m3[...], sep_ref[0:1, :]) - rr3
    x3[...] = r1[...]
    invert([m1], [x1], [r1], 4)
    ll2, lr2, rr2, l2, e2 = eliminate(x1, z1, y2_ref, size)
    right = m3[...] - rr2
    put_arc(
        arc_ref,
        x3[...] - ll2,
        -lr2,
        right,
        left_diagonal - diagonal_of(ll2),
        diagonal_of(right),
        target(0) - l1 - l2,
        target(4) - e3 - e2,
    )


def segment(tiles, inner, sep):
    size = tiles.shape[1]
    square = pltpu.VMEM((size, size), F32)
    couplings = jax.ShapeDtypeStruct((2 * size + PAD, size), F32)
    tall = pltpu.VMEM((2 * size + PAD, size), F32)
    return pl.pallas_call(
        segment_kernel,
        out_shape=[jax.ShapeDtypeStruct((2 * size + ARC_PAD, size), F32)] + [couplings] * 3,
        scratch_shapes=[square] * 6 + [tall] * 2,
        compiler_params=pltpu.CompilerParams(vmem_limit_bytes=VMEM_BYTES),
        name="segment",
    )(tiles, inner, sep)


def merge_kernel(right_ref, mine_ref, other_ref, arc_ref, y_ref, m, x, r, z):
    size = mine_ref.shape[1]
    is_right = right_ref[0] == 1

    def first(low, high):
        return jnp.where(is_right, other_ref[low:high, :], mine_ref[low:high, :])

    def second(low, high):
        return jnp.where(is_right, mine_ref[low:high, :], other_ref[low:high, :])

    end = 2 * size

    def row(side, k):
        return side(end + k, end + k + 1)

    half = lower_upper(second(0, size), first(0, size))
    m[...] = symmetric(half, row(first, 1) + row(second, 0))
    put_couplings(
        z, first(size, end), second(size, end).T, row(first, 3) + row(second, 2), size
    )
    invert([m], [x], [r], 3)
    ll, lr, rr, left, right = eliminate(x, z, y_ref, size)
    put_arc(
        arc_ref,
        first(0, size) - ll,
        -lr,
        second(0, size) - rr,
        row(first, 0) - diagonal_of(ll),
        row(second, 1) - diagonal_of(rr),
        row(first, 2) - left,
        row(second, 3) - right,
    )


def merge(is_right, mine, other):
    size = mine.shape[1]
    square = pltpu.VMEM((size, size), F32)
    vmem = pl.BlockSpec(memory_space=pltpu.VMEM)
    return pl.pallas_call(
        merge_kernel,
        in_specs=[pl.BlockSpec(memory_space=pltpu.SMEM), vmem, vmem],
        out_shape=[
            jax.ShapeDtypeStruct((2 * size + ARC_PAD, size), F32),
            jax.ShapeDtypeStruct((2 * size + PAD, size), F32),
        ],
        scratch_shapes=[square] * 3 + [pltpu.VMEM((2 * size + PAD, size), F32)],
        compiler_params=pltpu.CompilerParams(vmem_limit_bytes=VMEM_BYTES),
        name="merge",
    )(is_right, mine, other)


def finish_kernel(levels, bits_ref, arc_ref, *refs):
    merged = refs[:levels]
    y1_ref, y2_ref, y3_ref, sep_ref, inner_ref, m, x, r = refs[levels:]
    size = arc_ref.shape[1]
    end = 2 * size
    half = arc_ref[:size, :] + arc_ref[size:end, :]
    m[...] = symmetric(half, arc_ref[end : end + 1, :] + arc_ref[end + 1 : end + 2, :])
    invert([m], [x], [r], 3)

    def middle(y_ref, left, right):
        return (
            y_ref[2 * size : 2 * size + PAD, :]
            - mm_three(left, y_ref[:size, :])
            - mm_three(right, y_ref[size : 2 * size, :])
        )

    total = arc_ref[end + 2 : end + 3, :] + arc_ref[end + 3 : end + 4, :]
    top = mm_high(jnp.broadcast_to(total, (PAD, size)), x[...])
    left, right = top, top
    for level in range(levels - 1, -1, -1):
        between = middle(merged[level], left, right)
        between = jnp.broadcast_to(between[:1, :], (PAD, size))
        in_right = bits_ref[level] == 1
        left, right = jnp.where(in_right, between, left), jnp.where(in_right, right, between)
    step2 = jnp.broadcast_to(middle(y2_ref, left, right)[:1, :], (PAD, size))
    step1 = middle(y1_ref, left, step2)
    step3 = middle(y3_ref, step2, right)
    sep_ref[...] = right[:1, :]
    inner_ref[0:1, :] = step1[:1, :]
    inner_ref[1:2, :] = step2[:1, :]
    inner_ref[2:3, :] = step3[:1, :]


def finish(bits, arc, merged, inner):
    size = arc.shape[1]
    square = pltpu.VMEM((size, size), F32)
    vmem = pl.BlockSpec(memory_space=pltpu.VMEM)
    return pl.pallas_call(
        functools.partial(finish_kernel, len(merged)),
        in_specs=[pl.BlockSpec(memory_space=pltpu.SMEM)] + [vmem] * (1 + len(merged) + len(inner)),
        out_shape=[
            jax.ShapeDtypeStruct((1, size), F32),
            jax.ShapeDtypeStruct((len(inner), size), F32),
        ],
        scratch_shapes=[square] * 3,
        compiler_params=pltpu.CompilerParams(vmem_limit_bytes=VMEM_BYTES),
        name="finish",
    )(bits, arc, *merged, *inner)


def shards(jac_first, jac_second, residual, damp_inner, damp_sep):
    tiles = line_sum(gram(jac_first[0], jac_second[0], residual[0]), "band")
    arc, *inner = segment(tiles, damp_inner[0], damp_sep)
    count = lax.axis_size("seg")
    levels = count.bit_length() - 1
    here = lax.axis_index("seg")
    bits = jnp.stack([(here >> level) & 1 for level in range(levels)]).astype(jnp.int32)
    merged = []
    for level in range(levels):
        other = exchange(arc, "seg", level, "band")
        arc, saved = merge(bits[level : level + 1], arc, other)
        merged.append(saved)
    sep, steps = finish(bits, arc, merged, inner)
    return (sep, steps[None])


def solution(mesh):
    return jax.shard_map(
        shards,
        mesh=mesh,
        in_specs=(
            P("seg", None, "band", None),
            P("seg", None, "band", None),
            P("seg", None, "band"),
            P("seg", None, None),
            P("seg", None),
        ),
        out_specs=(P("seg", None), P("seg", None, None)),
        check_vma=False,
    )
```

```python
import functools

import jax
import jax.numpy as jnp
from jax import lax
from jax.experimental import pallas as pl
from jax.experimental.pallas import tpu as pltpu
from jax.sharding import PartitionSpec as P

HIGH = lax.Precision.HIGHEST
F32 = jnp.float32
BF16 = jnp.bfloat16
FINE_STEPS = 64
FINE_ENOUGH = 1e-6
PAD = 8
TAIL = 16
CHUNK = 56
ARC_PAD = 16
MIB = 1024 * 1024


def mm(left, right):
    return jnp.dot(left, right, preferred_element_type=F32)


def mm_high(left, right):
    return jnp.dot(left, right, precision=HIGH, preferred_element_type=F32)


def mm_high_t(left, right):
    return lax.dot_general(
        left, right, (((1,), (1,)), ((), ())), precision=HIGH, preferred_element_type=F32
    )


def eye_mask(size):
    rows = lax.broadcasted_iota(jnp.int32, (size, size), 0)
    columns = lax.broadcasted_iota(jnp.int32, (size, size), 1)
    return rows == columns


def plus_diagonal(matrix, row):
    return matrix + jnp.where(eye_mask(matrix.shape[0]), row, 0.0)


def diagonal_of(matrix):
    return jnp.sum(jnp.where(eye_mask(matrix.shape[0]), matrix, 0.0), axis=0, keepdims=True)


def lower_upper(low, up):
    size = low.shape[0]
    rows = lax.broadcasted_iota(jnp.int32, (size, size), 0)
    columns = lax.broadcasted_iota(jnp.int32, (size, size), 1)
    return jnp.where(rows > columns, low, jnp.where(rows < columns, up, 0.0))


def symmetric(half, diagonal):
    return plus_diagonal(half + half.T, diagonal)


def split(matrix):
    high = matrix.astype(BF16)
    return high, (matrix - high.astype(F32)).astype(BF16)


def mm_parts(left, right):
    return mm(
        jnp.concatenate([left[0], left[0], left[1]], axis=1),
        jnp.concatenate([right[0], right[1], right[0]], axis=0),
    )


def mm_parts_t(left, right):
    return lax.dot_general(
        jnp.concatenate([left[0], left[0], left[1]], axis=1),
        jnp.concatenate([right[0], right[1], right[0]], axis=1),
        (((1,), (1,)), ((), ())),
        preferred_element_type=F32,
    )


def mm_three(left, right):
    return mm_parts(split(left), split(right))


def invert(mats, invs, resids, coarse_steps):
    size = mats[0].shape[0]

    def start(m, x):
        scale = 1.0 / jnp.max(jnp.sum(jnp.abs(m[...]), axis=0, keepdims=True))
        x[...] = jnp.where(eye_mask(size), 2.0 * scale, 0.0) - (scale * scale) * m[...]

    def residuals(product):
        worst = None
        for m, x, r in zip(mats, invs, resids):
            r[...] = jnp.where(eye_mask(size), 1.0, 0.0) - product(m[...], x[...])
            one = jnp.sum(r[...] * r[...])
            worst = one if worst is None else jnp.maximum(worst, one)
        return worst

    for m, x in zip(mats, invs):
        start(m, x)

    @pl.loop(0, coarse_steps)
    def _(_):
        for m, x in zip(mats, invs):
            xb = x[...].astype(BF16)
            rb = jnp.where(eye_mask(size), 1.0, 0.0) - mm(m[...].astype(BF16), xb)
            x[...] += mm(xb, rb.astype(BF16))

    good = residuals(mm_three) < 0.25

    @pl.when(good)
    def _():
        for x, r in zip(invs, resids):
            x[...] += mm(x[...].astype(BF16), r[...].astype(BF16))

    @pl.when(jnp.logical_not(good))
    def _():
        for m, x in zip(mats, invs):
            start(m, x)

    def more(state):
        step, now = state
        return jnp.logical_and(step < FINE_STEPS, now > FINE_ENOUGH)

    def fine(state):
        step, _ = state
        for x, r in zip(invs, resids):
            x[...] += mm_high(x[...], r[...])
        return (step + 1, residuals(mm_high))

    lax.while_loop(more, fine, (jnp.int32(0), residuals(mm_high)))
    for x, r in zip(invs, resids):
        x[...] += mm(x[...].astype(BF16), r[...].astype(BF16))


def eliminate(inv, z, y, size):
    zs = split(z[...])
    y[...] = mm_parts(zs, split(inv[...]))
    ys = split(y[...])

    def rows(parts, low, high):
        return parts[0][low:high, :], parts[1][low:high, :]

    z_both, z_right = rows(zs, 0, 2 * size), rows(zs, size, 2 * size)
    y_left, y_right = rows(ys, 0, size), rows(ys, size, 2 * size)
    top = mm_parts_t(y_left, z_both)
    ll, lr = top[:, :size], top[:, size:]
    rr = mm_parts_t(y_right, z_right)
    solved = y[2 * size :, :]
    left = mm_high_t(solved, z[:size, :])
    right = mm_high_t(solved, z[size : 2 * size, :])
    return ll, lr, rr, left[:1, :], right[:1, :]


def put_couplings(z, from_left, from_right, target, size):
    z[:size, :] = from_left
    z[size : 2 * size, :] = from_right
    z[2 * size :, :] = jnp.zeros((PAD, size), F32)
    z[2 * size : 2 * size + 1, :] = target


def gram_kernel(first_ref, second_ref, resid_ref, out_ref, *, links, size):
    link = pl.program_id(0)
    first = first_ref[0]
    second = second_ref[0]
    both = jnp.concatenate([first, second], axis=1)
    at = first.T
    prod = mm(at, both)
    paa = prod[:, :size]
    pab = prod[:, size:]
    pbb = mm(second.T, second)
    grads = mm(resid_ref[...], both)
    which = lax.broadcasted_iota(jnp.int32, grads.shape, 0)
    grads = jnp.sum(jnp.where(which == link, grads, 0.0), axis=0, keepdims=True)
    grad_a = grads[:, :size]
    grad_b = grads[:, size:]
    third = size // 3
    strips = links // 2 * size
    offs = strips + 2 * third
    tail = offs + links * size
    added = pbb - pab - pab.T + paa

    @pl.when(link == 0)
    def _():
        out_ref[:offs, :] = jnp.zeros((offs, size), F32)
        out_ref[tail:, :] = jnp.zeros((TAIL, size), F32)

    out_ref[pl.ds(pl.multiple_of(offs + link * size, 8), size), :] = pab - paa
    for k in range(links):

        @pl.when(link == k)
        def _(k=k):
            low, up = (paa, added) if k % 2 == 0 else (0.0 * paa, paa)
            at = k // 2 * size
            out_ref[at : at + size, :] += lower_upper(low, up)
            at += size
            if k == links - 1:
                for strip, blocks in enumerate((((1, 0), (2, 0), (2, 1)), ((0, 0), (1, 1), (2, 2)))):
                    for place, (i, j) in enumerate(blocks):
                        out_ref[
                            at + strip * third : at + (strip + 1) * third,
                            place * third : (place + 1) * third,
                        ] = added[i * third : (i + 1) * third, j * third : (j + 1) * third]
            elif k % 2 == 1:
                out_ref[at : at + size, :] += lower_upper(added, 0.0 * paa)

    rows = lax.broadcasted_iota(jnp.int32, (TAIL, size), 0)
    out_ref[tail:, :] += (
        jnp.where(rows == link, diagonal_of(paa), 0.0)
        + jnp.where(rows == link + 1, diagonal_of(added), 0.0)
        + jnp.where(rows == link + PAD, grad_a, 0.0)
        + jnp.where(rows == link + PAD + 1, grad_b - grad_a, 0.0)
    )


def gram(first, second, resid):
    links, rows, size = first.shape
    height = (links // 2 + links) * size + 2 * (size // 3) + TAIL
    block = pl.BlockSpec((1, rows, size), lambda link: (link, 0, 0))
    return pl.pallas_call(
        functools.partial(gram_kernel, links=links, size=size),
        grid=(links,),
        in_specs=[block, block, pl.BlockSpec((links, rows), lambda link: (0, 0))],
        out_specs=pl.BlockSpec((height, size), lambda link: (0, 0)),
        out_shape=jax.ShapeDtypeStruct((height, size), F32),
        compiler_params=pltpu.CompilerParams(vmem_limit_bytes=24 * MIB),
        name="gram",
    )(first, second, resid)


def line_sum_kernel(axis, chunks, own, out, fl, fr, sr, sl, send_r, recv_r, send_l, recv_l):
    count = lax.axis_size(axis)
    me = lax.axis_index(axis)
    right, left = lax.rem(me + 1, count), lax.rem(me + count - 1, count)
    has_left, has_right = me > 0, me < count - 1
    barrier = pltpu.get_barrier_semaphore()

    @pl.when(has_left)
    def _():
        pl.semaphore_signal(
            barrier, inc=1, device_id={axis: left}, device_id_type=pl.DeviceIdType.MESH
        )

    @pl.when(has_right)
    def _():
        pl.semaphore_signal(
            barrier, inc=1, device_id={axis: right}, device_id_type=pl.DeviceIdType.MESH
        )

    @pl.when(jnp.logical_and(has_left, has_right))
    def _():
        pl.semaphore_wait(barrier, 2)

    @pl.when(jnp.logical_not(jnp.logical_and(has_left, has_right)))
    def _():
        pl.semaphore_wait(barrier, 1)

    def rows_of(chunk):
        return pl.ds(pl.multiple_of(chunk * CHUNK, 8), CHUNK)

    def copy(chunk, source, target, send, recv, device):
        rows = rows_of(chunk)
        return pltpu.make_async_remote_copy(
            src_ref=source.at[rows],
            dst_ref=target.at[rows],
            send_sem=send.at[chunk],
            recv_sem=recv.at[chunk],
            device_id={axis: device},
            device_id_type=pl.DeviceIdType.MESH,
        )

    def to_right(chunk):
        return copy(chunk, sr, fl, send_r, recv_r, right)

    def to_left(chunk):
        return copy(chunk, sl, fr, send_l, recv_l, left)

    def pass_on(chunk, there, source, came, has_in, has_out):
        rows = rows_of(chunk)

        @pl.when(has_in)
        def _():
            there(chunk).wait_recv()

        @pl.when(jnp.logical_and(has_in, has_out))
        def _():
            source[rows, :] = own[rows, :] + came[rows, :]
            there(chunk).start()

        @pl.when(jnp.logical_and(jnp.logical_not(has_in), has_out))
        def _():
            source[rows, :] = own[rows, :]
            there(chunk).start()

    def go_right(chunk):
        pass_on(chunk, to_right, sr, fl, has_left, has_right)

    def go_left(chunk):
        pass_on(chunk, to_left, sl, fr, has_right, has_left)

    near_left = 2 * me < count
    ahead = jnp.where(near_left, count - 1 - 2 * me, 2 * me + 1 - count)
    lag = 2 * ahead

    def step(i, carry):
        @pl.when(jnp.logical_and(i < chunks, near_left))
        def _():
            go_right(i)

        @pl.when(jnp.logical_and(i < chunks, jnp.logical_not(near_left)))
        def _():
            go_left(i)

        late = jnp.maximum(i - lag, 0)
        due = jnp.logical_and(i >= lag, i < chunks + lag)

        @pl.when(jnp.logical_and(due, near_left))
        def _():
            go_left(late)

        @pl.when(jnp.logical_and(due, jnp.logical_not(near_left)))
        def _():
            go_right(late)

        @pl.when(due)
        def _():
            rows = rows_of(late)

            @pl.when(jnp.logical_and(has_left, has_right))
            def _():
                out[rows, :] = fl[rows, :] + own[rows, :] + fr[rows, :]

            @pl.when(jnp.logical_not(has_left))
            def _():
                out[rows, :] = own[rows, :] + fr[rows, :]

            @pl.when(jnp.logical_not(has_right))
            def _():
                out[rows, :] = fl[rows, :] + own[rows, :]

        return carry

    lax.fori_loop(0, chunks + 2 * (count - 1), step, 0)

    def settle(chunk, carry):
        @pl.when(has_right)
        def _():
            to_right(chunk).wait_send()

        @pl.when(has_left)
        def _():
            to_left(chunk).wait_send()

        return carry

    lax.fori_loop(0, chunks, settle, 0)


def line_sum(own, axis):
    height, size = own.shape
    chunks = height // CHUNK
    assert height == chunks * CHUNK and lax.axis_size(axis) > 1
    return pl.pallas_call(
        functools.partial(line_sum_kernel, axis, chunks),
        in_specs=[pl.BlockSpec(memory_space=pltpu.VMEM)],
        out_specs=pl.BlockSpec(memory_space=pltpu.VMEM),
        out_shape=jax.ShapeDtypeStruct(own.shape, F32),
        scratch_shapes=[pltpu.VMEM(own.shape, F32)] * 4 + [pltpu.SemaphoreType.DMA((chunks,))] * 4,
        compiler_params=pltpu.CompilerParams(
            collective_id=0, has_side_effects=True, vmem_limit_bytes=28 * MIB
        ),
        name="line_sum",
    )(own)


def exchange_kernel(axis, bit, twin_axis, chunks, arc, out, land, send_a, recv_a, send_b, recv_b):
    me = lax.axis_index(axis)
    place = lax.axis_index(twin_axis)
    partner = me + bit - 2 * bit * ((me // bit) % 2)
    twin = place + 1 - 2 * (place % 2)
    base = (place % 2) * (chunks * CHUNK)
    barrier = pltpu.get_barrier_semaphore()
    for peer in ({axis: partner}, {twin_axis: twin}):
        pl.semaphore_signal(barrier, inc=1, device_id=peer, device_id_type=pl.DeviceIdType.MESH)
    pl.semaphore_wait(barrier, 2)

    def copy(chunk, source, send, recv, peer):
        rows = pl.ds(pl.multiple_of(base + chunk * CHUNK, 8), CHUNK)
        return pltpu.make_async_remote_copy(
            src_ref=source.at[rows],
            dst_ref=land.at[rows],
            send_sem=send.at[chunk],
            recv_sem=recv.at[chunk],
            device_id=peer,
            device_id_type=pl.DeviceIdType.MESH,
        )

    across = [copy(k, arc, send_a, recv_a, {axis: partner}) for k in range(chunks)]
    along = [copy(k, land, send_b, recv_b, {twin_axis: twin}) for k in range(chunks)]
    for one in across:
        one.start()
    for one, two in zip(across, along):
        one.wait_recv()
        two.start()
    for one, two in zip(across, along):
        two.wait_recv()
        one.wait_send()
        two.wait_send()
    out[...] = land[...]


def exchange(arc, axis, level, twin_axis):
    count, twins = lax.axis_size(axis), lax.axis_size(twin_axis)
    bit = 1 << level
    if level == 0 or twins % 2:
        return lax.ppermute(arc, axis, [(i, i ^ bit) for i in range(count)])
    chunks = arc.shape[0] // (2 * CHUNK)
    assert arc.shape[0] == 2 * chunks * CHUNK
    return pl.pallas_call(
        functools.partial(exchange_kernel, axis, bit, twin_axis, chunks),
        in_specs=[pl.BlockSpec(memory_space=pltpu.VMEM)],
        out_specs=pl.BlockSpec(memory_space=pltpu.VMEM),
        out_shape=jax.ShapeDtypeStruct(arc.shape, F32),
        scratch_shapes=[pltpu.VMEM(arc.shape, F32)] + [pltpu.SemaphoreType.DMA((chunks,))] * 4,
        compiler_params=pltpu.CompilerParams(
            collective_id=1 + level, has_side_effects=True, vmem_limit_bytes=16 * MIB
        ),
        name=f"exchange_{level}",
    )(arc)


def put_arc(arc_ref, left, lr, right, left_diagonal, right_diagonal, l, r):
    size = lr.shape[0]
    end = 2 * size
    arc_ref[:size, :] = lower_upper(left, right)
    arc_ref[size:end, :] = lr
    arc_ref[end:, :] = jnp.zeros((ARC_PAD, size), F32)
    for k, row in enumerate((left_diagonal, right_diagonal, l, r)):
        arc_ref[end + k : end + k + 1, :] = row


def segment_kernel(
    tiles_ref, inner_ref, sep_ref, arc_ref, y1_ref, y2_ref, y3_ref, m1, m3, x1, x3, r1, r3, z1, z3
):
    size = tiles_ref.shape[1]

    third = size // 3
    offs = 2 * size + 2 * third
    tail = offs + 4 * size

    def square(k):
        return tiles_ref[k * size : (k + 1) * size, :]

    def off(k):
        return tiles_ref[offs + k * size : offs + (k + 1) * size, :]

    def strip(k, place):
        at = 2 * size + k * third
        return tiles_ref[at : at + third, place * third : (place + 1) * third]

    def put_last(ref):
        for place, (i, j) in enumerate(((1, 0), (2, 0), (2, 1))):
            block = strip(0, place)
            ref[i * third : (i + 1) * third, j * third : (j + 1) * third] = block
            ref[j * third : (j + 1) * third, i * third : (i + 1) * third] = block.T
            ref[place * third : (place + 1) * third, place * third : (place + 1) * third] = strip(
                1, place
            )

    def diagonal(k):
        return tiles_ref[tail + k : tail + k + 1, :]

    def target(k):
        return -tiles_ref[tail + PAD + k : tail + PAD + k + 1, :]

    m1[...] = symmetric(lower_upper(jnp.zeros((size, size), F32), square(0)), diagonal(1) + inner_ref[0:1, :])
    m3[...] = symmetric(lower_upper(jnp.zeros((size, size), F32), square(1)), diagonal(3) + inner_ref[2:3, :])
    put_couplings(z1, off(0), off(1).T, target(1), size)
    put_couplings(z3, off(2), off(3).T, target(3), size)
    invert([m1, m3], [x1, x3], [r1, r3], 4)
    ll1, lr1, rr1, l1, e1 = eliminate(x1, z1, y1_ref, size)
    m1[...] = symmetric(lower_upper(square(1), jnp.zeros((size, size), F32)), diagonal(2) + inner_ref[1:2, :]) - rr1
    z1[:size, :] = -lr1
    r1[...] = square(0) - ll1
    left_diagonal = diagonal(0) - diagonal_of(ll1)
    ll3, lr3, rr3, l3, e3 = eliminate(x3, z3, y3_ref, size)
    m1[...] -= ll3
    put_couplings(z1, z1[:size, :], -lr3.T, target(2) - e1 - l3, size)
    put_last(m3)
    m3[...] = plus_diagonal(m3[...], sep_ref[0:1, :]) - rr3
    x3[...] = r1[...]
    invert([m1], [x1], [r1], 4)
    ll2, lr2, rr2, l2, e2 = eliminate(x1, z1, y2_ref, size)
    right = m3[...] - rr2
    put_arc(
        arc_ref,
        x3[...] - ll2,
        -lr2,
        right,
        left_diagonal - diagonal_of(ll2),
        diagonal_of(right),
        target(0) - l1 - l2,
        target(4) - e3 - e2,
    )


def segment(tiles, inner, sep):
    size = tiles.shape[1]
    square = pltpu.VMEM((size, size), F32)
    couplings = jax.ShapeDtypeStruct((2 * size + PAD, size), F32)
    tall = pltpu.VMEM((2 * size + PAD, size), F32)
    return pl.pallas_call(
        segment_kernel,
        out_shape=[jax.ShapeDtypeStruct((2 * size + ARC_PAD, size), F32)] + [couplings] * 3,
        scratch_shapes=[square] * 6 + [tall] * 2,
        compiler_params=pltpu.CompilerParams(vmem_limit_bytes=30 * MIB),
        name="segment",
    )(tiles, inner, sep)


def merge_kernel(right_ref, mine_ref, other_ref, arc_ref, y_ref, m, x, r, z):
    size = mine_ref.shape[1]
    is_right = right_ref[0] == 1

    def first(low, high):
        return jnp.where(is_right, other_ref[low:high, :], mine_ref[low:high, :])

    def second(low, high):
        return jnp.where(is_right, mine_ref[low:high, :], other_ref[low:high, :])

    end = 2 * size

    def row(side, k):
        return side(end + k, end + k + 1)

    half = lower_upper(second(0, size), first(0, size))
    m[...] = symmetric(half, row(first, 1) + row(second, 0))
    put_couplings(
        z, first(size, end), second(size, end).T, row(first, 3) + row(second, 2), size
    )
    invert([m], [x], [r], 3)
    ll, lr, rr, left, right = eliminate(x, z, y_ref, size)
    put_arc(
        arc_ref,
        first(0, size) - ll,
        -lr,
        second(0, size) - rr,
        row(first, 0) - diagonal_of(ll),
        row(second, 1) - diagonal_of(rr),
        row(first, 2) - left,
        row(second, 3) - right,
    )


def merge(is_right, mine, other):
    size = mine.shape[1]
    square = pltpu.VMEM((size, size), F32)
    vmem = pl.BlockSpec(memory_space=pltpu.VMEM)
    return pl.pallas_call(
        merge_kernel,
        in_specs=[pl.BlockSpec(memory_space=pltpu.SMEM), vmem, vmem],
        out_shape=[
            jax.ShapeDtypeStruct((2 * size + ARC_PAD, size), F32),
            jax.ShapeDtypeStruct((2 * size + PAD, size), F32),
        ],
        scratch_shapes=[square] * 3 + [pltpu.VMEM((2 * size + PAD, size), F32)],
        compiler_params=pltpu.CompilerParams(vmem_limit_bytes=24 * MIB),
        name="merge",
    )(is_right, mine, other)


def finish_kernel(levels, bits_ref, arc_ref, *refs):
    merged = refs[:levels]
    y1_ref, y2_ref, y3_ref, sep_ref, inner_ref, m, x, r = refs[levels:]
    size = arc_ref.shape[1]
    end = 2 * size
    half = arc_ref[:size, :] + arc_ref[size:end, :]
    m[...] = symmetric(half, arc_ref[end : end + 1, :] + arc_ref[end + 1 : end + 2, :])
    invert([m], [x], [r], 3)

    def middle(y_ref, left, right):
        return (
            y_ref[2 * size : 2 * size + PAD, :]
            - mm_three(left, y_ref[:size, :])
            - mm_three(right, y_ref[size : 2 * size, :])
        )

    total = arc_ref[end + 2 : end + 3, :] + arc_ref[end + 3 : end + 4, :]
    top = mm_high(jnp.broadcast_to(total, (PAD, size)), x[...])
    left, right = top, top
    for level in range(levels - 1, -1, -1):
        between = middle(merged[level], left, right)
        between = jnp.broadcast_to(between[:1, :], (PAD, size))
        in_right = bits_ref[level] == 1
        left, right = jnp.where(in_right, between, left), jnp.where(in_right, right, between)
    step2 = jnp.broadcast_to(middle(y2_ref, left, right)[:1, :], (PAD, size))
    step1 = middle(y1_ref, left, step2)
    step3 = middle(y3_ref, step2, right)
    sep_ref[...] = right[:1, :]
    inner_ref[0:1, :] = step1[:1, :]
    inner_ref[1:2, :] = step2[:1, :]
    inner_ref[2:3, :] = step3[:1, :]


def finish(bits, arc, merged, inner):
    size = arc.shape[1]
    square = pltpu.VMEM((size, size), F32)
    vmem = pl.BlockSpec(memory_space=pltpu.VMEM)
    return pl.pallas_call(
        functools.partial(finish_kernel, len(merged)),
        in_specs=[pl.BlockSpec(memory_space=pltpu.SMEM)] + [vmem] * (1 + len(merged) + len(inner)),
        out_shape=[
            jax.ShapeDtypeStruct((1, size), F32),
            jax.ShapeDtypeStruct((len(inner), size), F32),
        ],
        scratch_shapes=[square] * 3,
        compiler_params=pltpu.CompilerParams(vmem_limit_bytes=24 * MIB),
        name="finish",
    )(bits, arc, *merged, *inner)


def shards(jac_first, jac_second, residual, damp_inner, damp_sep):
    tiles = line_sum(gram(jac_first[0], jac_second[0], residual[0]), "band")
    arc, *inner = segment(tiles, damp_inner[0], damp_sep)
    count = lax.axis_size("seg")
    levels = count.bit_length() - 1
    here = lax.axis_index("seg")
    bits = jnp.stack([(here >> level) & 1 for level in range(levels)]).astype(jnp.int32)
    merged = []
    for level in range(levels):
        other = exchange(arc, "seg", level, "band")
        arc, saved = merge(bits[level : level + 1], arc, other)
        merged.append(saved)
    sep, steps = finish(bits, arc, merged, inner)
    return (sep, steps[None])


def solution(mesh):
    return jax.shard_map(
        shards,
        mesh=mesh,
        in_specs=(
            P("seg", None, "band", None),
            P("seg", None, "band", None),
            P("seg", None, "band"),
            P("seg", None, None),
            P("seg", None),
        ),
        out_specs=(P("seg", None), P("seg", None, None)),
        check_vma=False,
    )
```
